32 devices in a mesh: col: 8 (over z, y), ch: 4 (over x, core).
Axes of the slice: x: 2, y: 2, z: 4, core: 2. Of those that a mesh axis runs over, the one named last changes fastest.
Arguments:
- features: bfloat16 [64, 8, 8, 1024], P('ch', None, 'col'), may hold values from -6 to 6
- solid_mask: int32 [8, 8, 1024], P(None, 'col'), may hold values 0 or 1
- weight_one: bfloat16 [64, 27, 64], P('ch'), may hold values from -0.15625 to 0.15625
- bias_one: float32 [64], P('ch'), may hold values from -3 to 3
- weight_two: bfloat16 [64, 27, 64], P('ch'), may hold values from -0.15625 to 0.15625
- bias_two: float32 [64], P('ch'), may hold values from -3 to 3
Outputs:
- activations: bfloat16 [64, 8, 8, 1024], P('ch', None, 'col')
The draws below stay inside these ranges and needn't reach their ends.
All inputs are finite; a program needn't handle non-finite values. No bound on the sum of `solid_mask` on one device may be relied on, other than what follows from the above.
Results may differ from the reference program's by a relative error of at most 0.013.
Values may be sent and summed in bfloat16 or wider, within the bound.
No kernel may reach another device: no remote copies, remote signals or barrier semaphores. Data moves between devices by JAX's collectives and lax.ppermute only.
A program may use at most 64 MiB of HBM per device.

```python
import jax
import jax.numpy as jnp
from jax import lax

C = 64
X = 8
CY = 32
CZ = 32
TAPS = 27
GZ = 8
GY = 1
COLS = 8
CELLS = 1024


def place_ends(drawn, stream_key, least, largest):
    place = [jax.random.randint(jax.random.fold_in(stream_key, axis), (), 0, length) for axis, length in enumerate(drawn.shape)]
    main_axis = drawn.shape.index(max(drawn.shape))
    neighbour = place[:main_axis] + [(place[main_axis] + 1) % drawn.shape[main_axis]] + place[main_axis + 1:]
    return drawn.at[tuple(place)].set(least).at[tuple(neighbour)].set(largest)


def shard_levels(key, dims, pieces, least, top_value):
    loudness, own = 1.0, jax.random.fold_in(key, 6)
    for dim, parts in pieces:
        steps = jnp.exp(jax.random.uniform(jax.random.fold_in(own, dim), (parts,), jnp.float32, least / len(pieces), top_value / len(pieces)))
        loudness = loudness * jnp.repeat(steps, dims[dim] // parts).reshape([-1 if axis == dim else 1 for axis in range(len(dims))])
    return loudness


def centred(key, shape, width, most, cuts=(), kind=jnp.bfloat16):
    entries = width * jax.random.normal(key, shape, jnp.float32)
    if cuts:
        entries = entries * shard_levels(key, shape, cuts, -0.22, 0.18)
    return jnp.clip(entries, -most, most).astype(kind)


def setup_inputs(seed: int = 0) -> dict:
    key_of = jax.random.split(jax.random.key(seed), 7)
    features = centred(key_of[0], (C, X, COLS, CELLS), 1.0, 6.0, ((0, 4), (2, 8)))
    solid_mask = place_ends((jax.random.randint(key_of[1], (X, COLS, CELLS), 0, 4) < 1).astype(jnp.int32), jax.random.fold_in(key_of[1], 1), 0, 1)
    weight_one = centred(key_of[2], (C, TAPS, C), (TAPS * C) ** -0.5, 0.15625, ((0, 4),))
    bias_one = centred(key_of[3], (C,), 0.5, 3.0, ((0, 4),), jnp.float32)
    weight_two = centred(key_of[4], (C, TAPS, C), (TAPS * C) ** -0.5, 0.15625, ((0, 4),))
    bias_two = centred(key_of[5], (C,), 0.5, 3.0, ((0, 4),), jnp.float32)
    return dict(features=features, solid_mask=solid_mask, weight_one=weight_one, bias_one=bias_one, weight_two=weight_two, bias_two=bias_two)


def to_grid(field):
    depth = field.shape[0]
    shaped = field.reshape(depth, X, GY, GZ, CY, CZ).transpose(0, 1, 2, 4, 3, 5)
    return shaped.reshape(depth, X, GY * CY, GZ * CZ)


def from_grid(field):
    depth = field.shape[0]
    shaped = field.reshape(depth, X, GY, CY, GZ, CZ).transpose(0, 1, 2, 4, 3, 5)
    return shaped.reshape(depth, X, GY * GZ, CY * CZ)


def convolve(field, weight):
    outputs = weight.shape[0]
    inputs = weight.shape[2]
    kernel = weight.astype(jnp.float32).reshape(outputs, 3, 3, 3, inputs).transpose(0, 4, 1, 2, 3)
    result = lax.conv_general_dilated(field.astype(jnp.float32)[None], kernel, (1, 1, 1), "SAME",
                                      dimension_numbers=("NCDHW", "OIDHW", "NCDHW"),
                                      precision=lax.Precision.HIGHEST)
    return result[0]


def reference(features, solid_mask, weight_one, bias_one, weight_two, bias_two):
    open_cells = to_grid((1 - solid_mask).astype(jnp.float32)[None])[0]
    gridded = to_grid(features)
    hidden = jnp.maximum(convolve(gridded, weight_one) + bias_one[:, None, None, None], 0.0) * open_cells[None]
    hidden = hidden.astype(jnp.bfloat16)
    second = jnp.maximum(convolve(hidden, weight_two) + bias_two[:, None, None, None], 0.0) * open_cells[None]
    return from_grid(second.astype(jnp.bfloat16))
```

```python
import functools

import jax
import jax.numpy as jnp
import numpy as np
from jax import lax
from jax.experimental import pallas as pl
from jax.experimental.pallas import tpu as pltpu
from jax.sharding import PartitionSpec as P

CY = 32
CZ = 32
PITCH = CZ + 4
BF = jnp.bfloat16
F32 = jnp.float32


def frame_sources(rows, lanes):
    sources = np.full(lanes, -1)
    for lane in range(PITCH * (CY + 2 * rows)):
        y, z = lane // PITCH - rows, lane % PITCH - 2
        if 0 <= y < CY:
            if 0 <= z < CZ:
                sources[lane] = CZ * y + z
            elif z >= CZ:
                sources[lane] = 1024 + 2 * y + z - CZ
            else:
                sources[lane] = 1024 + 64 + 2 * y + z + 2
        elif rows == 2:
            sources[lane] = 1024 + (128 + PITCH * (y + 2) if y < 0 else 256 + PITCH * (y - CY)) + z + 2
    return sources


def windows(sources, limit, tile=256):
    spans = []
    for start in range(0, len(sources), tile):
        part = sources[start : start + tile]
        part = part[(part >= 0) & (part < limit)]
        low = int(part.min()) // 128 * 128 if len(part) else 0
        high = -(-(int(part.max()) + 1) // 128) * 128 if len(part) else 128
        spans.append((start, min(tile, len(sources) - start), low, high))
    return spans


def one_hot(sources, count):
    return (np.arange(count)[:, None] == sources[None, :]).astype(np.float32)


def dot(a, b):
    return jnp.dot(a, b, preferred_element_type=F32)


def roll(x, shift):
    n = x.shape[1]
    return x if shift % n == 0 else pltpu.roll(x, (-shift) % n, 1)


def swap_rows(outer, inner):
    row = lax.broadcasted_iota(jnp.int32, (128, 128), 0)
    col = lax.broadcasted_iota(jnp.int32, (128, 128), 1)
    return ((row % outer) * inner + row // outer == col).astype(F32).astype(BF)


def pack_kernel(f_ref, mask_ref, select_ref, halo_ref):
    opened = jnp.concatenate([(1 - mask_ref[x]).astype(F32) for x in range(8)] + [jnp.zeros((8, 1024), F32)], 0)
    halo_ref[0:128] = dot(f_ref[...], select_ref[...]).astype(BF)
    halo_ref[128:144] = dot(opened.astype(BF), select_ref[...]).astype(BF)


def main_kernel(rows, spans, back, me_ref, f0, f1, f2, f3, h0, h1, h2, h3, w0, w1, w2, w3, mask_ref, mask_halo, own, bias_ref,
                frame_ref, halo_frame_ref, back_ref, out_ref, field, hidden, first, second, bias_one, opened, last):
    lanes = opened.shape[1]
    me = me_ref[0]
    to_plane = swap_rows(16, 8)
    zero = jnp.zeros((192, lanes), BF)
    field[0:192] = zero
    field[9 * 192 : 10 * 192] = zero
    hidden[0:64] = zero[0:64]
    hidden[9 * 64 : 10 * 64] = zero[0:64]

    def framed(cells, halo):
        parts = []
        for start, size, low, high in spans:
            part = dot(halo, halo_frame_ref[:, start : start + size])
            part += dot(cells[:, low:high], frame_ref[low:high, start : start + size])
            parts.append(part)
        return jnp.concatenate(parts, 1)

    cells_open = jnp.concatenate([(1 - mask_ref[x]).astype(F32) for x in range(8)] + [jnp.zeros((8, 1024), F32)], 0)
    opened[...] = framed(cells_open.astype(BF), mask_halo[...])

    for k, (f, h, w) in enumerate(((f0, h0, w0), (f1, h1, w1), (f2, h2, w2), (f3, h3, w3))):
        base = pl.multiple_of((me ^ k) * 16, 16)
        planes = dot(to_plane, framed(f[...], h[...]).astype(BF))
        for e in range(3):
            moved = roll(planes, e - 1).astype(BF)
            for x in range(8):
                field[pl.ds(192 * (x + 1) + 64 * e + base, 16)] = moved[16 * x : 16 * x + 16]

        def tap(t):
            block = w[16 * (t % 14) : 16 * (t % 14) + 16]
            return block[:, 0:64] if t < 14 else block[:, 64:128]

        blank = jnp.zeros((16, 192), BF)
        for b in range(3):
            taps = [tap(9 * a + 3 * b + e) for a in range(3) for e in range(3)]
            first[pl.ds(128 * b + base, 16)] = jnp.concatenate(taps + [blank], 1)
            first[pl.ds(128 * b + 64 + base, 16)] = jnp.concatenate([blank] + taps, 1)
        tail = w[16 * 13 : 16 * 14].astype(F32)
        total = tail[:, 64:65] + tail[:, 65:66] + tail[:, 66:67]
        bias_one[pl.ds(base, 16)] = jnp.broadcast_to(total, (16, 128))

    blank = jnp.zeros((16, 64), BF)
    for b in range(3):
        for e in range(3):
            taps = [own[9 * a + 3 * b + e] for a in range(3)]
            row = 32 * (3 * b + e)
            second[row : row + 16] = jnp.concatenate(taps + [blank], 1)
            second[row + 16 : row + 32] = jnp.concatenate([blank] + taps, 1)

    column = bias_one[:, 0:1]
    for q in range(4):
        sums = dot(first[...], field[384 * q : 384 * q + 768])
        total = roll(sums[0:128], -PITCH) + sums[128:256] + roll(sums[256:384], PITCH)
        for half in range(2):
            x = 2 * q + half
            value = jnp.maximum(total[64 * half : 64 * half + 64] + column, 0.0) * opened[x : x + 1]
            hidden[64 * (x + 1) : 64 * (x + 2)] = value.astype(BF)

    column = jnp.broadcast_to(bias_ref[...], (16, 128))[:, 0:1]
    for q in range(4):
        sums = dot(second[...], hidden[128 * q : 128 * q + 256])
        total = sums[32 * 4 : 32 * 5]
        for b in range(3):
            for e in range(3):
                if (b, e) != (1, 1):
                    row = 32 * (3 * b + e)
                    total += roll(sums[row : row + 32], PITCH * (b - 1) + e - 1)
        for half in range(2):
            x = 2 * q + half
            value = jnp.maximum(total[16 * half : 16 * half + 16] + column, 0.0) * opened[x : x + 1]
            last[16 * x : 16 * x + 16] = value.astype(BF)

    parts = [dot(last[:, low:high], back_ref[low:high, start : start + size]) for start, size, low, high in back]
    cells = jnp.concatenate(parts, 1).astype(BF)
    out_ref[...] = dot(swap_rows(8, 16), cells).astype(BF)


def on_device(features, solid_mask, weight_one, bias_one, weight_two, bias_two):
    columns = lax.axis_size("col")
    grid_z = min(8, columns)
    grid_y = columns // grid_z
    rows = 1 if grid_y == 1 else 2
    lanes = -(-PITCH * (CY + 2 * rows) // 128) * 128
    me = lax.axis_index("ch").astype(jnp.int32).reshape(1)

    def across(v, bit):
        return lax.ppermute(v, "ch", [(i, i ^ bit) for i in range(lax.axis_size("ch"))])

    def along_z(v, step):
        route = [(c, c + step) for c in range(columns) if 0 <= c % grid_z + step < grid_z]
        return lax.ppermute(v, "col", route)

    def along_y(v, step):
        route = [(c, c + step * grid_z) for c in range(columns) if 0 <= c // grid_z + step < grid_y]
        return lax.ppermute(v, "col", route)

    cells = features.reshape(128, 1024)
    far = across(cells, 2)
    near = across(cells, 1)

    taps = weight_one.transpose(1, 0, 2)
    high = bias_one.astype(BF)
    rest = bias_one - high.astype(F32)
    middle = rest.astype(BF)
    low = (rest - middle.astype(F32)).astype(BF)
    terms = jnp.pad(jnp.stack([high, middle, low], 1), ((0, 0), (0, 61)))
    weights = jnp.concatenate([taps[:14], jnp.concatenate([taps[14:], terms[None]], 0)], 2).reshape(224, 128)

    edge = np.array([32 * (n // 2) + n % 2 + (30 if n >= 64 else 0) - (1024 if n >= 64 else 0) for n in range(128)])
    select = jnp.asarray(one_hot(edge, 1024), BF)
    rims = pl.pallas_call(
        pack_kernel,
        out_shape=jax.ShapeDtypeStruct((144, 128), BF),
        compiler_params=pltpu.CompilerParams(vmem_limit_bytes=32 << 20),
        name="pack",
    )(cells, solid_mask, select)
    after, before = along_z(rims, -1), along_z(rims, 1)
    side = lax.broadcasted_iota(jnp.int32, (144, 128), 1)
    halo = jnp.where(side < 64, after, before)
    if grid_y > 1:
        opened = (1 - solid_mask).astype(BF).reshape(8, 1024)
        whole = jnp.concatenate([cells, opened, jnp.zeros((8, 1024), BF)], 0).reshape(144, CY, CZ)
        upper = halo[:, :64].reshape(144, CY, 2)
        lower = halo[:, 64:].reshape(144, CY, 2)
        wide = jnp.concatenate([lower, whole, upper], 2)
        south = along_y(wide[:, CY - 2 :], 1).reshape(144, 2 * PITCH)
        north = along_y(wide[:, :2], -1).reshape(144, 2 * PITCH)
        edges = [jnp.pad(v, ((0, 0), (0, 128 - 2 * PITCH))) for v in (south, north)]
        halo = jnp.concatenate([halo] + edges, 1)
    mask_halo = halo[128:]
    halo = halo[:128]

    halo_far, weights_far = across(halo, 2), across(weights, 2)
    halo_near, weights_near = across(halo, 1), across(weights, 1)
    cross = across(far, 1)
    halo_cross, weights_cross = across(halo_far, 1), across(weights_far, 1)

    sources = frame_sources(rows, lanes)
    frame = jnp.asarray(one_hot(sources, 1024), BF)
    halo_frame = jnp.asarray(one_hot(sources - 1024, halo.shape[1]), BF)
    back_sources = np.array([PITCH * (n // CZ + rows) + n % CZ + 2 for n in range(1024)])
    back = jnp.asarray(one_hot(back_sources, lanes), BF)

    vmem = pl.BlockSpec(memory_space=pltpu.VMEM)
    result = pl.pallas_call(
        functools.partial(main_kernel, rows, windows(sources, 1024), windows(back_sources, lanes)),
        out_shape=jax.ShapeDtypeStruct((128, 1024), BF),
        in_specs=[pl.BlockSpec(memory_space=pltpu.SMEM)] + [vmem] * 19,
        out_specs=vmem,
        scratch_shapes=[
            pltpu.VMEM((10 * 192, lanes), BF),
            pltpu.VMEM((10 * 64, lanes), BF),
            pltpu.VMEM((384, 768), BF),
            pltpu.VMEM((288, 256), BF),
            pltpu.VMEM((64, 128), F32),
            pltpu.VMEM((16, lanes), F32),
            pltpu.VMEM((128, lanes), BF),
        ],
        compiler_params=pltpu.CompilerParams(vmem_limit_bytes=48 << 20),
        name="layers",
    )(
        me, cells, near, far, cross, halo, halo_near, halo_far, halo_cross,
        weights, weights_near, weights_far, weights_cross, solid_mask, mask_halo,
        weight_two.transpose(1, 0, 2), bias_two.reshape(16, 1), frame, halo_frame, back,
    )
    return result.reshape(16, 8, 1, 1024)


def solution(mesh):
    in_specs = (
        P("ch", None, "col", None),
        P(None, "col", None),
        P("ch", None, None),
        P("ch"),
        P("ch", None, None),
        P("ch"),
    )
    out_specs = P("ch", None, "col", None)
    return jax.shard_map(
        on_device, mesh=mesh, in_specs=in_specs, out_specs=out_specs, check_vma=False
    )
```

```python
import jax
import jax.numpy as jnp
from jax import lax
from jax.experimental import pallas as pl
from jax.experimental.pallas import tpu as pltpu
from jax.sharding import PartitionSpec as P

CY = 32
CZ = 32
BF = jnp.bfloat16
F32 = jnp.float32
WHOLE = 63000000


def iota(shape, dimension):
    return lax.broadcasted_iota(jnp.int32, shape, dimension)


def dot(a, b):
    return jnp.dot(a, b, preferred_element_type=F32)


def roll(x, shift):
    n = x.shape[1]
    return x if shift % n == 0 else pltpu.roll(x, (-shift) % n, 1)


def swap_rows(outer, inner):
    row, col = iota((128, 128), 0), iota((128, 128), 1)
    return jnp.where((row % outer) * inner + row // outer == col, 1.0, 0.0).astype(BF)


def pick_columns(zs):
    lane = iota((8, 128), 1)[0:1]
    group = lane >> 5
    z = jnp.where(group == 0, zs[0], jnp.where(group == 1, zs[1], jnp.where(group == 2, zs[2], zs[3])))
    return jnp.where(iota((CY * CZ, 128), 0) == (lane & 31) * CZ + z, 1.0, 0.0).astype(BF)


def with_neighbours(outer, inner):
    lane = iota(outer.shape, 1)
    middle = jnp.where(
        lane < 64,
        jnp.where(lane < 32, roll(outer, 32), roll(inner, -32)),
        jnp.where(lane < 96, roll(inner, 32), roll(outer, -32)),
    )
    return jnp.where(lane < 64, outer, inner), middle, jnp.where(lane < 64, inner, outer)


def fetch(sources, targets, sems):
    copies = [pltpu.make_async_copy(s, t, sems.at[k]) for k, (s, t) in enumerate(zip(sources, targets))]
    for copy in copies:
        copy.start()
    return copies


def open_cells(mask):
    return jnp.concatenate([(1 - mask[x]).astype(F32) for x in range(8)], 0)


def bias_column(bias, shape):
    row = iota(shape, 0)
    column = jnp.zeros(shape, F32)
    for o in range(16):
        column = jnp.where(row == o, bias[o], column)
    return column


def first_kernel(f_hbm, mask_hbm, one_hbm, bias_hbm, rims, weights, f, mask, one, bias, sems):
    copies = fetch((one_hbm, bias_hbm, mask_hbm, f_hbm), (one, bias, mask, f), sems)
    select = pick_columns((30, 31, 0, 1))
    place = iota((16, 64), 1)
    copies[0].wait()
    copies[1].wait()
    column = bias_column(bias, (16, 64))
    high = column.astype(BF).astype(F32)
    middle = (column - high).astype(BF).astype(F32)
    terms = jnp.where(place == 0, high, jnp.where(place == 1, middle, jnp.where(place == 2, column - high - middle, 0.0)))
    for t in range(14):
        other = one[t + 14] if t < 13 else terms.astype(BF)
        weights[16 * t : 16 * t + 16] = jnp.concatenate([one[t], other], 1)
    copies[2].wait()
    opened = jnp.concatenate([open_cells(mask), jnp.zeros((8, CY * CZ), F32)], 0)
    rims[128:144] = dot(opened.astype(BF), select).astype(BF)
    copies[3].wait()
    rims[0:128] = dot(f[...], select).astype(BF)


def place_inputs(base, f, w, field, first, bias_one):
    planes = dot(swap_rows(16, 8), f[...])
    for e in range(3):
        moved = roll(planes, e - 1).astype(BF)
        for x in range(8):
            field[pl.ds(192 * (x + 1) + 64 * e + base, 16)] = moved[16 * x : 16 * x + 16]

    def tap(t):
        block = w[16 * (t % 14) : 16 * (t % 14) + 16]
        return block[:, 0:64] if t < 14 else block[:, 64:128]

    blank = jnp.zeros((16, 192), BF)
    for b in range(3):
        taps = [tap(9 * a + 3 * b + e) for a in range(3) for e in range(3)]
        first[pl.ds(128 * b + base, 16)] = jnp.concatenate(taps + [blank], 1)
        first[pl.ds(128 * b + 64 + base, 16)] = jnp.concatenate([blank] + taps, 1)
    tail = w[16 * 13 : 16 * 14].astype(F32)
    total = tail[:, 64:65] + tail[:, 65:66] + tail[:, 66:67]
    bias_one[pl.ds(base, 16)] = jnp.broadcast_to(total, (16, 128))


def near_kernel(me_ref, bias, f0, f1, w0, w1, mask, two, field, first, bias_one, opened, second, bias_two):
    field[0:192] = jnp.zeros((192, CY * CZ), BF)
    field[9 * 192 : 10 * 192] = jnp.zeros((192, CY * CZ), BF)
    opened[...] = open_cells(mask)
    me = me_ref[0]
    for k, (f, w) in enumerate(((f0, w0), (f1, w1))):
        place_inputs(pl.multiple_of((me ^ k) * 16, 16), f, w, field, first, bias_one)
    blank = jnp.zeros((16, 64), BF)
    for e in range(3):
        for b in range(3):
            taps = [two[9 * a + 3 * b + e] for a in range(3)]
            row = 96 * e + 32 * b
            second[row : row + 16] = jnp.concatenate(taps + [blank], 1)
            second[row + 16 : row + 32] = jnp.concatenate([blank] + taps, 1)
    bias_two[...] = bias_column(bias, (16, 128))


def inside():
    lane = iota((8, CY * CZ), 1)[0:1]
    return jnp.where(lane >= CZ, 1.0, 0.0), jnp.where(lane < (CY - 1) * CZ, 1.0, 0.0)


def one_kernel(me_ref, f2, f3, w2, w3, opened, field_in, first_in, bias_in,
               field, first, bias_one, hidden, rims, open_rims):
    del field_in, first_in, bias_in
    me = me_ref[0]
    for k, (f, w) in enumerate(((f2, w2), (f3, w3))):
        place_inputs(pl.multiple_of((me ^ (2 + k)) * 16, 16), f, w, field, first, bias_one)

    after_first, before_last = inside()
    hidden[0:64] = jnp.zeros((64, CY * CZ), BF)
    hidden[9 * 64 : 10 * 64] = jnp.zeros((64, CY * CZ), BF)
    column = bias_one[:, 0:1]
    for q in range(4):
        sums = dot(first[...], field[384 * q : 384 * q + 768])
        total = roll(sums[0:128], -CZ) * after_first + sums[128:256] + roll(sums[256:384], CZ) * before_last
        for half in range(2):
            x = 2 * q + half
            value = jnp.maximum(total[64 * half : 64 * half + 64] + column, 0.0) * opened[x : x + 1]
            hidden[64 * (x + 1) : 64 * (x + 2)] = value.astype(BF)

    select = pick_columns((0, 1, 30, 31))
    for x in range(8):
        rims[64 * x : 64 * x + 64] = dot(field[192 * (x + 1) + 64 : 192 * (x + 1) + 128], select).astype(BF)
    open_rims[...] = dot(opened[...].astype(BF), select)


def two_kernel(hidden, second, bias_two, opened, out_ref, inner, last):
    after_first, before_last = inside()
    column = bias_two[:, 0:1]
    for q in range(4):
        sums = dot(second[...], hidden[128 * q : 128 * q + 256])
        moved = [sum(roll(sums[96 * e + 32 * b : 96 * e + 32 * b + 32], e - 1) for e in range(3)) for b in range(3)]
        total = roll(moved[0], -CZ) * after_first + moved[1] + roll(moved[2], CZ) * before_last
        for half in range(2):
            x = 2 * q + half
            value = jnp.maximum(total[16 * half : 16 * half + 16] + column, 0.0) * opened[x : x + 1]
            last[16 * x : 16 * x + 16] = value.astype(BF)
    out_ref[...] = dot(swap_rows(8, 16), last[...]).astype(BF)
    inner[...] = dot(hidden[64 : 9 * 64], pick_columns((1, 2, 29, 30))).astype(BF)


def edge_kernel(me_ref, h0, h1, h2, h3, mask_halo, rims, inner, open_rims, first, bias_one, second, bias_two, out_in,
                out_ref, halo, field, hidden, last):
    me = me_ref[0]
    to_plane = swap_rows(16, 8)
    for k, h in enumerate((h0, h1, h2, h3)):
        base = pl.multiple_of((me ^ k) * 16, 16)
        planes = dot(to_plane, h[...]).astype(BF)
        for x in range(8):
            halo[pl.ds(64 * x + base, 16)] = planes[16 * x : 16 * x + 16]

    field[0:192] = jnp.zeros((192, 128), BF)
    field[9 * 192 : 10 * 192] = jnp.zeros((192, 128), BF)
    hidden[:, 0:64] = jnp.zeros((3, 64, 128), BF)
    hidden[:, 9 * 64 : 10 * 64] = jnp.zeros((3, 64, 128), BF)
    for e, moved in enumerate(with_neighbours(halo[...].astype(F32), rims[...].astype(F32))):
        moved = moved.astype(BF)
        for x in range(8):
            field[192 * (x + 1) + 64 * e : 192 * (x + 1) + 64 * e + 64] = moved[64 * x : 64 * x + 64]
    opened = with_neighbours(mask_halo[0:8].astype(F32), open_rims[...])[1]

    y = iota((8, 128), 1)[0:1] & 31
    after_first = jnp.where(y > 0, 1.0, 0.0)
    before_last = jnp.where(y < CY - 1, 1.0, 0.0)
    column = bias_one[:, 0:1]
    for q in range(4):
        sums = dot(first[...], field[384 * q : 384 * q + 768])
        total = roll(sums[0:128], -1) * after_first + sums[128:256] + roll(sums[256:384], 1) * before_last
        for half in range(2):
            x = 2 * q + half
            value = jnp.maximum(total[64 * half : 64 * half + 64] + column, 0.0) * opened[x : x + 1]
            between = inner[64 * x : 64 * x + 64].astype(F32)
            for e, moved in enumerate(with_neighbours(value.astype(BF).astype(F32), between)):
                hidden[e, 64 * (x + 1) : 64 * (x + 2)] = moved.astype(BF)

    column = bias_two[:, 0:1]
    for q in range(4):
        sums = dot(second[0:96], hidden[0, 128 * q : 128 * q + 256])
        for e in (1, 2):
            sums += dot(second[96 * e : 96 * e + 96], hidden[e, 128 * q : 128 * q + 256])
        total = roll(sums[0:32], -1) * after_first + sums[32:64] + roll(sums[64:96], 1) * before_last
        for half in range(2):
            x = 2 * q + half
            value = jnp.maximum(total[16 * half : 16 * half + 16] + column, 0.0) * open_rims[x : x + 1]
            last[16 * x : 16 * x + 16] = value.astype(BF)

    cell = iota((8, CY * CZ), 1)[0:1]
    z = cell & 31
    group = jnp.where(z < 2, z, z - 28)
    row = jnp.where((z < 2) | (z >= 30), 32 * group + (cell >> 5), -1)
    spread = jnp.where(iota((128, CY * CZ), 0) == row, 1.0, 0.0).astype(BF)
    edges = dot(swap_rows(8, 16), dot(last[...], spread).astype(BF))
    out_ref[...] = jnp.where(row >= 0, edges, out_in[...].astype(F32)).astype(BF)


def cost(micros):
    return pl.CostEstimate(flops=int(micros * 1.15e9), bytes_accessed=int(micros * 3e6), transcendentals=0)


def one_row(features, solid_mask, weight_one, bias_one, weight_two, bias_two):
    columns = lax.axis_size("col")
    me = lax.axis_index("ch").astype(jnp.int32).reshape(1)

    def across(v, bit):
        return lax.ppermute(v, "ch", [(i, i ^ bit) for i in range(lax.axis_size("ch"))])

    def after(v, other):
        return lax.optimization_barrier((v, other))[0]

    def exchange(v, parity):
        route = []
        for c in range(parity, columns - 1, 2):
            route += [(c, c + 1), (c + 1, c)]
        return lax.ppermute(v, "col", route)

    smem = pl.BlockSpec(memory_space=pltpu.SMEM)
    hbm = pl.BlockSpec(memory_space=pltpu.HBM)
    vmem = pl.BlockSpec(memory_space=pltpu.VMEM)
    mask_buffer = pltpu.VMEM((8, 1, 1024), jnp.int32)
    weight_buffer = pltpu.VMEM((27, 16, 64), BF)
    cell_buffer = pltpu.VMEM((128, 1024), BF)
    bias_buffer = pltpu.SMEM((16,), F32)
    shape = jax.ShapeDtypeStruct

    cells = features.reshape(128, 1024)
    far = across(cells, 2)
    near = across(cells, 1)
    rims, weights = pl.pallas_call(
        first_kernel,
        out_shape=[shape((144, 128), BF), shape((224, 128), BF)],
        in_specs=[hbm] * 4,
        out_specs=[vmem] * 2,
        scratch_shapes=[cell_buffer, mask_buffer, weight_buffer, bias_buffer, pltpu.SemaphoreType.DMA((4,))],
        compiler_params=pltpu.CompilerParams(vmem_limit_bytes=WHOLE),
        cost_estimate=cost(1),
        name="first",
    )(cells, solid_mask, weight_one.transpose(1, 0, 2), bias_one)

    odd = exchange(rims, 1)
    even = exchange(after(rims, near), 0)
    weights_far, weights_near = across(weights, 2), across(weights, 1)
    cross = across(far, 1)

    kept = [shape((1920, 1024), BF), shape((384, 768), BF), shape((64, 128), F32)]
    field, first, bias, opened, second, bias_second = pl.pallas_call(
        near_kernel,
        out_shape=kept + [shape((8, 1024), F32), shape((288, 256), BF), shape((16, 128), F32)],
        in_specs=[smem, smem] + [vmem] * 6,
        out_specs=[vmem] * 6,
        compiler_params=pltpu.CompilerParams(vmem_limit_bytes=16 << 20),
        cost_estimate=cost(1.5),
        name="near",
    )(me, bias_two, cells, near, weights, weights_near, solid_mask, weight_two.transpose(1, 0, 2))

    odd, even, opened = lax.optimization_barrier((odd, even, opened))
    is_odd = lax.axis_index("col") % 2 == 1
    side = lax.broadcasted_iota(jnp.int32, (144, 128), 1)
    halo = jnp.where((side < 64) == is_odd, even, odd)
    mask_halo = halo[128:]
    halo = halo[:128]
    weights_cross = across(after(weights_far, halo), 1)
    halo_far = across(halo, 2)

    _, first, bias, hidden, rim_cells, open_rims = pl.pallas_call(
        one_kernel,
        out_shape=kept + [shape((640, 1024), BF), shape((512, 128), BF), shape((8, 128), F32)],
        in_specs=[smem] + [vmem] * 8,
        out_specs=[vmem] * 6,
        input_output_aliases={6: 0, 7: 1, 8: 2},
        compiler_params=pltpu.CompilerParams(vmem_limit_bytes=24 << 20),
        cost_estimate=cost(4),
        name="one",
    )(me, far, cross, weights_far, weights_cross, opened, field, first, bias)

    halo_near = across(halo, 1)
    halo_cross = across(after(halo_far, open_rims), 1)

    out, inner = pl.pallas_call(
        two_kernel,
        out_shape=[shape((128, 1024), BF), shape((512, 128), BF)],
        in_specs=[vmem] * 4,
        out_specs=[vmem] * 2,
        scratch_shapes=[pltpu.VMEM((128, 1024), BF)],
        compiler_params=pltpu.CompilerParams(vmem_limit_bytes=16 << 20),
        cost_estimate=cost(2),
        name="two",
    )(hidden, second, bias_second, opened)

    result = pl.pallas_call(
        edge_kernel,
        out_shape=shape((128, 1024), BF),
        in_specs=[smem] + [vmem] * 13,
        out_specs=vmem,
        scratch_shapes=[
            pltpu.VMEM((512, 128), BF),
            pltpu.VMEM((1920, 128), BF),
            pltpu.VMEM((3, 640, 128), BF),
            pltpu.VMEM((128, 128), BF),
        ],
        compiler_params=pltpu.CompilerParams(vmem_limit_bytes=16 << 20),
        cost_estimate=cost(2),
        name="edge",
    )(me, halo, halo_near, halo_far, halo_cross, mask_halo, rim_cells, inner, open_rims, first, bias, second, bias_second, out)
    return result.reshape(16, 8, 1, 1024)


def passed_along(block, axis, distance):
    devices = range(lax.axis_size(axis))
    route = [(i - distance, i) for i in devices if i - distance in devices]
    return lax.ppermute(block, axis, route)


def kernel_of(weight):
    outputs = weight.shape[0]
    inputs = weight.shape[2]
    return weight.reshape(outputs, 3, 3, 3, inputs).transpose(0, 4, 1, 2, 3)


def many_rows(features, solid_mask, weight_one, bias_one, weight_two, bias_two):
    cells = features.shape[3]
    columns = lax.axis_size("col")
    grid_z = min(8, columns)
    open_cells = (1 - solid_mask).astype(jnp.float32)

    def pad_columns(field):
        depth = field.shape[0]
        depth_x = field.shape[1]
        cube = field.reshape(depth, depth_x, CY, CZ)
        below = passed_along(cube[:, :, :, CZ - 1 :], "col", 1)
        above = passed_along(cube[:, :, :, :1], "col", -1)
        place = lax.axis_index("col") % grid_z
        below = jnp.where(place > 0, below, jnp.zeros_like(below))
        above = jnp.where(place < grid_z - 1, above, jnp.zeros_like(above))
        cube = jnp.concatenate([below, cube, above], axis=3)
        south = passed_along(cube[:, :, CY - 1 :, :], "col", grid_z)
        north = passed_along(cube[:, :, :1, :], "col", -grid_z)
        return jnp.concatenate([south, cube, north], axis=2)

    def pad_planes(framed):
        return jnp.pad(framed, ((0, 0), (1, 1), (0, 0), (0, 0)))

    def padded_inputs(field):
        whole = lax.all_gather(field, "ch", axis=0, tiled=True)
        framed = pad_columns(whole)
        return pad_planes(framed)

    def convolve(framed, weight):
        depth_x = framed.shape[1] - 2
        result = lax.conv_general_dilated(
            framed[None],
            kernel_of(weight),
            (1, 1, 1),
            "VALID",
            dimension_numbers=("NCDHW", "OIDHW", "NCDHW"),
            preferred_element_type=jnp.float32,
        )
        return result[0].reshape(weight.shape[0], depth_x, 1, cells)

    def finish(total, bias, opened):
        return (jnp.maximum(total + bias[:, None, None, None], 0.0) * opened[None]).astype(
            jnp.bfloat16
        )

    hidden = finish(convolve(padded_inputs(features), weight_one), bias_one, open_cells)
    total = convolve(padded_inputs(hidden), weight_two)
    return finish(total, bias_two, open_cells)


def on_device(*arguments):
    columns = lax.axis_size("col")
    return one_row(*arguments) if columns <= 8 and columns % 2 == 0 else many_rows(*arguments)


def solution(mesh):
    in_specs = (
        P("ch", None, "col", None),
        P(None, "col", None),
        P("ch", None, None),
        P("ch"),
        P("ch", None, None),
        P("ch"),
    )
    out_specs = P("ch", None, "col", None)
    return jax.shard_map(
        on_device, mesh=mesh, in_specs=in_specs, out_specs=out_specs, check_vma=False
    )
```

```python
import jax
import jax.numpy as jnp
from jax import lax
from jax.experimental import pallas as pl
from jax.experimental.pallas import tpu as pltpu
from jax.sharding import PartitionSpec as P

CY = 32
CZ = 32
BF = jnp.bfloat16
F32 = jnp.float32
SELECT = 5


def iota(shape, dimension):
    return lax.broadcasted_iota(jnp.int32, shape, dimension)


def dot(a, b):
    return jnp.dot(a, b, preferred_element_type=F32)


def roll(x, shift):
    n = x.shape[1]
    return x if shift % n == 0 else pltpu.roll(x, (-shift) % n, 1)


def swap_rows(outer, inner):
    row, col = iota((128, 128), 0), iota((128, 128), 1)
    return jnp.where((row % outer) * inner + row // outer == col, 1.0, 0.0).astype(BF)


def pick_columns(zs):
    lane = iota((8, 128), 1)[0:1]
    group = lane >> 5
    z = jnp.where(group == 0, zs[0], jnp.where(group == 1, zs[1], jnp.where(group == 2, zs[2], zs[3])))
    return jnp.where(iota((CY * CZ, 128), 0) == (lane & 31) * CZ + z, 1.0, 0.0).astype(BF)


def with_neighbours(outer, inner):
    lane = iota(outer.shape, 1) & 127
    middle = jnp.where(
        lane < 64,
        jnp.where(lane < 32, roll(outer, 32), roll(inner, -32)),
        jnp.where(lane < 96, roll(inner, 32), roll(outer, -32)),
    )
    return jnp.where(lane < 64, outer, inner), middle, jnp.where(lane < 64, inner, outer)


def open_cells(mask):
    return jnp.concatenate([(1 - mask[x]).astype(F32) for x in range(8)], 0)


def bias_column(bias, shape):
    row = iota(shape, 0)
    column = jnp.zeros(shape, F32)
    for o in range(16):
        column = jnp.where(row == o, bias[o], column)
    return column


def select_kernel(out):
    out[...] = pick_columns((30, 31, 0, 1))


def first_kernel(bias, select, f, mask, one, rims, weights):
    rims[0:128] = dot(f[...], select[...]).astype(BF)
    opened = jnp.concatenate([open_cells(mask), jnp.zeros((8, CY * CZ), F32)], 0)
    rims[128:144] = dot(opened.astype(BF), select[...]).astype(BF)
    place = iota((16, 64), 1)
    column = bias_column(bias, (16, 64))
    high = column.astype(BF).astype(F32)
    middle = (column - high).astype(BF).astype(F32)
    terms = jnp.where(place == 0, high, jnp.where(place == 1, middle, jnp.where(place == 2, column - high - middle, 0.0)))
    for t in range(14):
        other = one[t + 14] if t < 13 else terms.astype(BF)
        weights[16 * t : 16 * t + 16] = jnp.concatenate([one[t], other], 1)


def place_features(base, f, field, rims):
    planes = dot(swap_rows(16, 8), f[...])
    rim = dot(planes.astype(BF), pick_columns((0, 1, 30, 31))).astype(BF)
    for x in range(8):
        rims[pl.ds(64 * x + base, 16)] = rim[16 * x : 16 * x + 16]
    for e in range(3):
        moved = roll(planes, e - 1).astype(BF)
        for x in range(8):
            field[pl.ds(192 * (x + 1) + 64 * e + base, 16)] = moved[16 * x : 16 * x + 16]


def place_filters(base, w, first, bias_one):
    def tap(t):
        block = w[16 * (t % 14) : 16 * (t % 14) + 16]
        return block[:, 0:64] if t < 14 else block[:, 64:128]

    blank = jnp.zeros((16, 192), BF)
    for b in range(3):
        taps = [tap(9 * a + 3 * b + e) for a in range(3) for e in range(3)]
        first[pl.ds(128 * b + base, 16)] = jnp.concatenate(taps + [blank], 1)
        first[pl.ds(128 * b + 64 + base, 16)] = jnp.concatenate([blank] + taps, 1)
    tail = w[16 * 13 : 16 * 14].astype(F32)
    total = tail[:, 64:65] + tail[:, 65:66] + tail[:, 66:67]
    bias_one[pl.ds(base, 16)] = jnp.broadcast_to(total, (16, 128))


def near_kernel(me_ref, bias, f0, f1, mask, two, field, rims, opened, open_rims, second, bias_two):
    field[0:192] = jnp.zeros((192, CY * CZ), BF)
    field[9 * 192 : 10 * 192] = jnp.zeros((192, CY * CZ), BF)
    cells = open_cells(mask)
    opened[...] = cells
    open_rims[...] = dot(cells.astype(BF), pick_columns((0, 1, 30, 31)))
    me = me_ref[0]
    for k, f in enumerate((f0, f1)):
        place_features(pl.multiple_of((me ^ k) * 16, 16), f, field, rims)
    blank = jnp.zeros((16, 64), BF)
    for e in range(3):
        for b in range(3):
            taps = [two[9 * a + 3 * b + e] for a in range(3)]
            row = 96 * e + 32 * b
            second[row : row + 16] = jnp.concatenate(taps + [blank], 1)
            second[row + 16 : row + 32] = jnp.concatenate([blank] + taps, 1)
    bias_two[...] = bias_column(bias, (16, 128))


def far_kernel(me_ref, f2, field_in, rims_in, field, rims):
    del field_in, rims_in
    place_features(pl.multiple_of((me_ref[0] ^ 2) * 16, 16), f2, field, rims)


def inside():
    lane = iota((8, CY * CZ), 1)[0:1]
    return jnp.where(lane >= CZ, 1.0, 0.0), jnp.where(lane < (CY - 1) * CZ, 1.0, 0.0)


def one_kernel(me_ref, f3, w0, w1, w2, w3, opened, field_in, rims_in, field, rims, hidden, first, bias_one):
    del field_in, rims_in
    me = me_ref[0]
    for k, w in enumerate((w0, w1, w2, w3)):
        place_filters(pl.multiple_of((me ^ k) * 16, 16), w, first, bias_one)
    place_features(pl.multiple_of((me ^ 3) * 16, 16), f3, field, rims)

    after_first, before_last = inside()
    z = iota((8, CY * CZ), 1)[0:1] & 31
    settled = jnp.where((z > 0) & (z < CZ - 1), 1.0, 0.0)
    hidden[0:64] = jnp.zeros((64, CY * CZ), BF)
    hidden[9 * 64 : 10 * 64] = jnp.zeros((64, CY * CZ), BF)
    column = bias_one[:, 0:1]
    for q in range(4):
        sums = dot(first[...], field[384 * q : 384 * q + 768])
        total = roll(sums[0:128], -CZ) * after_first + sums[128:256] + roll(sums[256:384], CZ) * before_last
        for half in range(2):
            x = 2 * q + half
            value = jnp.maximum(total[64 * half : 64 * half + 64] + column, 0.0) * (opened[x : x + 1] * settled)
            hidden[64 * (x + 1) : 64 * (x + 2)] = value.astype(BF)


def two_kernel(me_ref, h0, h1, h23, mask_halo, rims, open_rims, first, bias_one, second, bias_two, opened, hidden,
               out_ref, halo, field, edge, terms, last):
    me = me_ref[0]
    to_plane = swap_rows(16, 8)
    for k, h in enumerate((h0, h1, h23.at[0:128], h23.at[128:256])):
        base = pl.multiple_of((me ^ k) * 16, 16)
        planes = dot(to_plane, h[...]).astype(BF)
        for x in range(8):
            halo[pl.ds(64 * x + base, 16)] = planes[16 * x : 16 * x + 16]

    def windows(x):
        return [(q, x + 1 - 2 * q) for q in range(4) if 0 <= x + 1 - 2 * q < 4]

    field[0:192, 0:128] = jnp.zeros((192, 128), BF)
    field[576:768, 384:512] = jnp.zeros((192, 128), BF)
    for e, moved in enumerate(with_neighbours(halo[...].astype(F32), rims[...].astype(F32))):
        moved = moved.astype(BF)
        for x in range(8):
            for q, place in windows(x):
                field[192 * place + 64 * e : 192 * place + 64 * e + 64, 128 * q : 128 * q + 128] = moved[64 * x : 64 * x + 64]
    open_edge = with_neighbours(mask_halo[0:8].astype(F32), open_rims[...])[1]

    y = iota((8, 512), 1)[0:1] & 31
    after_first = jnp.where(y > 0, 1.0, 0.0)
    before_last = jnp.where(y < CY - 1, 1.0, 0.0)
    sums = dot(first[...], field[...])
    total = roll(sums[0:128], -1) * after_first + sums[128:256] + roll(sums[256:384], 1) * before_last
    edge[0:64, 0:128] = jnp.zeros((64, 128), BF)
    edge[192:256, 384:512] = jnp.zeros((64, 128), BF)
    for half in range(2):
        opening = jnp.concatenate([open_edge[2 * q + half : 2 * q + half + 1] for q in range(4)], 1)
        value = jnp.maximum(total[64 * half : 64 * half + 64] + bias_one[:, 0:1], 0.0) * opening
        value = value.astype(BF)
        for k in range(4):
            for q, place in windows(2 * k + half):
                edge[64 * place : 64 * place + 64, 128 * q : 128 * q + 128] = value[:, 128 * k : 128 * k + 128]

    sums = dot(second[...], edge[...])
    before, same, behind = [
        roll(sums[r : r + 32], -1) * after_first + sums[r + 32 : r + 64] + roll(sums[r + 64 : r + 96], 1) * before_last
        for r in (0, 96, 192)
    ]
    lane = iota((32, 512), 1) & 127
    total = jnp.where(lane < 64, before, behind)
    total += jnp.where(lane < 32, roll(same, 32), jnp.where(lane < 96, 0.0, roll(same, -32)))
    high = total.astype(BF)
    low = (total - high.astype(F32)).astype(BF)
    for q in range(4):
        terms[32 * q : 32 * q + 32] = high[:, 128 * q : 128 * q + 128]
        terms[128 + 32 * q : 160 + 32 * q] = low[:, 128 * q : 128 * q + 128]
    cell = iota((8, CY * CZ), 1)[0:1]
    z = cell & 31
    row = jnp.where((z < 2) | (z >= 30), 32 * jnp.where(z < 2, z, z - 28) + (cell >> 5), -1)
    spread = jnp.where(iota((128, CY * CZ), 0) == row, 1.0, 0.0).astype(BF)

    after_first, before_last = inside()
    for q in range(4):
        sums = dot(second[...], hidden[128 * q : 128 * q + 256])
        moved = [sum(roll(sums[96 * e + 32 * b : 96 * e + 32 * b + 32], e - 1) for e in range(3)) for b in range(3)]
        total = roll(moved[0], -CZ) * after_first + moved[1] + roll(moved[2], CZ) * before_last
        total += dot(terms[32 * q : 32 * q + 32], spread) + dot(terms[128 + 32 * q : 160 + 32 * q], spread)
        for half in range(2):
            x = 2 * q + half
            value = jnp.maximum(total[16 * half : 16 * half + 16] + bias_two[:, 0:1], 0.0) * opened[x : x + 1]
            last[16 * x : 16 * x + 16] = value.astype(BF)
    out_ref[...] = dot(swap_rows(8, 16), last[...]).astype(BF)


def cost(micros):
    return pl.CostEstimate(flops=int(micros * 1.15e9), bytes_accessed=int(micros * 3e6), transcendentals=0)


def one_row(features, solid_mask, weight_one, bias_one, weight_two, bias_two):
    columns = lax.axis_size("col")
    me = lax.axis_index("ch").astype(jnp.int32).reshape(1)

    def across(v, bit):
        return lax.ppermute(v, "ch", [(i, i ^ bit) for i in range(lax.axis_size("ch"))])

    def after(v, other):
        return lax.optimization_barrier((v, other))[0]

    def exchange(v, parity):
        route = []
        for c in range(parity, columns - 1, 2):
            route += [(c, c + 1), (c + 1, c)]
        return lax.ppermute(v, "col", route)

    smem = pl.BlockSpec(memory_space=pltpu.SMEM)
    vmem = pl.BlockSpec(memory_space=pltpu.VMEM)
    shape = jax.ShapeDtypeStruct

    cells = features.reshape(128, 1024)
    far = across(cells, 2)
    near = across(cells, 1)
    select = pl.pallas_call(
        select_kernel,
        out_shape=shape((1024, 128), BF),
        out_specs=vmem,
        compiler_params=pltpu.CompilerParams(vmem_limit_bytes=4 << 20),
        cost_estimate=cost(SELECT),
        name="select",
    )()
    rims, weights = pl.pallas_call(
        first_kernel,
        out_shape=[shape((144, 128), BF), shape((224, 128), BF)],
        in_specs=[smem] + [vmem] * 4,
        out_specs=[vmem] * 2,
        compiler_params=pltpu.CompilerParams(vmem_limit_bytes=8 << 20),
        cost_estimate=cost(1),
        name="first",
    )(bias_one, select, cells, solid_mask, weight_one.transpose(1, 0, 2))

    odd = exchange(rims, 1)
    even = exchange(rims, 0)
    weights_far, weights_near = across(weights, 2), across(weights, 1)

    field_shape, rims_shape = shape((1920, 1024), BF), shape((512, 128), BF)
    field, rim_cells, opened, open_rims, second, bias_second = pl.pallas_call(
        near_kernel,
        out_shape=[field_shape, rims_shape, shape((8, 1024), F32), shape((8, 128), F32), shape((288, 256), BF), shape((16, 128), F32)],
        in_specs=[smem, smem] + [vmem] * 4,
        out_specs=[vmem] * 6,
        compiler_params=pltpu.CompilerParams(vmem_limit_bytes=16 << 20),
        cost_estimate=cost(0.1),
        name="near",
    )(me, bias_two, cells, near, solid_mask, weight_two.transpose(1, 0, 2))

    far = after(far, open_rims)
    cross = across(far, 1)
    field, rim_cells = pl.pallas_call(
        far_kernel,
        out_shape=[field_shape, rims_shape],
        in_specs=[smem] + [vmem] * 3,
        out_specs=[vmem] * 2,
        input_output_aliases={2: 0, 3: 1},
        compiler_params=pltpu.CompilerParams(vmem_limit_bytes=16 << 20),
        cost_estimate=cost(0.1),
        name="far",
    )(me, far, field, rim_cells)
    weights_far, rim_cells = lax.optimization_barrier((weights_far, rim_cells))
    weights_cross = across(weights_far, 1)

    odd, even, opened = lax.optimization_barrier((odd, even, opened))
    is_odd = lax.axis_index("col") % 2 == 1
    side = lax.broadcasted_iota(jnp.int32, (144, 128), 1)
    halo = jnp.where((side < 64) == is_odd, even, odd)
    mask_halo = halo[128:]
    halo = halo[:128]
    halo_near = across(halo, 1)
    halo_here, rim_cells = lax.optimization_barrier((jnp.concatenate([halo, halo_near], 0), rim_cells))
    halo_there = across(halo_here, 2)

    _, rim_cells, hidden, first, bias = pl.pallas_call(
        one_kernel,
        out_shape=[field_shape, rims_shape, shape((640, 1024), BF), shape((384, 768), BF), shape((64, 128), F32)],
        in_specs=[smem] + [vmem] * 8,
        out_specs=[vmem] * 5,
        input_output_aliases={7: 0, 8: 1},
        compiler_params=pltpu.CompilerParams(vmem_limit_bytes=24 << 20),
        cost_estimate=cost(4),
        name="one",
    )(me, cross, weights, weights_near, weights_far, weights_cross, opened, field, rim_cells)

    result = pl.pallas_call(
        two_kernel,
        out_shape=shape((128, 1024), BF),
        in_specs=[smem] + [vmem] * 12,
        out_specs=vmem,
        scratch_shapes=[
            pltpu.VMEM((512, 128), BF),
            pltpu.VMEM((768, 512), BF),
            pltpu.VMEM((256, 512), BF),
            pltpu.VMEM((256, 128), BF),
            pltpu.VMEM((128, 1024), BF),
        ],
        compiler_params=pltpu.CompilerParams(vmem_limit_bytes=16 << 20),
        cost_estimate=cost(3),
        name="two",
    )(me, halo, halo_near, halo_there, mask_halo, rim_cells, open_rims, first, bias, second, bias_second, opened, hidden)
    return result.reshape(16, 8, 1, 1024)


def passed_along(block, axis, distance):
    devices = range(lax.axis_size(axis))
    route = [(i - distance, i) for i in devices if i - distance in devices]
    return lax.ppermute(block, axis, route)


def kernel_of(weight):
    outputs = weight.shape[0]
    inputs = weight.shape[2]
    return weight.reshape(outputs, 3, 3, 3, inputs).transpose(0, 4, 1, 2, 3)


def many_rows(features, solid_mask, weight_one, bias_one, weight_two, bias_two):
    cells = features.shape[3]
    columns = lax.axis_size("col")
    grid_z = min(8, columns)
    open_cells = (1 - solid_mask).astype(jnp.float32)

    def pad_columns(field):
        depth = field.shape[0]
        depth_x = field.shape[1]
        cube = field.reshape(depth, depth_x, CY, CZ)
        below = passed_along(cube[:, :, :, CZ - 1 :], "col", 1)
        above = passed_along(cube[:, :, :, :1], "col", -1)
        place = lax.axis_index("col") % grid_z
        below = jnp.where(place > 0, below, jnp.zeros_like(below))
        above = jnp.where(place < grid_z - 1, above, jnp.zeros_like(above))
        cube = jnp.concatenate([below, cube, above], axis=3)
        south = passed_along(cube[:, :, CY - 1 :, :], "col", grid_z)
        north = passed_along(cube[:, :, :1, :], "col", -grid_z)
        return jnp.concatenate([south, cube, north], axis=2)

    def pad_planes(framed):
        return jnp.pad(framed, ((0, 0), (1, 1), (0, 0), (0, 0)))

    def padded_inputs(field):
        whole = lax.all_gather(field, "ch", axis=0, tiled=True)
        framed = pad_columns(whole)
        return pad_planes(framed)

    def convolve(framed, weight):
        depth_x = framed.shape[1] - 2
        result = lax.conv_general_dilated(
            framed[None],
            kernel_of(weight),
            (1, 1, 1),
            "VALID",
            dimension_numbers=("NCDHW", "OIDHW", "NCDHW"),
            preferred_element_type=jnp.float32,
        )
        return result[0].reshape(weight.shape[0], depth_x, 1, cells)

    def finish(total, bias, opened):
        return (jnp.maximum(total + bias[:, None, None, None], 0.0) * opened[None]).astype(
            jnp.bfloat16
        )

    hidden = finish(convolve(padded_inputs(features), weight_one), bias_one, open_cells)
    total = convolve(padded_inputs(hidden), weight_two)
    return finish(total, bias_two, open_cells)


def on_device(*arguments):
    columns = lax.axis_size("col")
    return one_row(*arguments) if columns <= 8 and columns % 2 == 0 else many_rows(*arguments)


def solution(mesh):
    in_specs = (
        P("ch", None, "col", None),
        P(None, "col", None),
        P("ch", None, None),
        P("ch"),
        P("ch", None, None),
        P("ch"),
    )
    out_specs = P("ch", None, "col", None)
    return jax.shard_map(
        on_device, mesh=mesh, in_specs=in_specs, out_specs=out_specs, check_vma=False
    )
```

```python
import jax
import jax.numpy as jnp
from jax import lax
from jax.experimental import pallas as pl
from jax.experimental.pallas import tpu as pltpu
from jax.sharding import PartitionSpec as P

CY = 32
CZ = 32
BF = jnp.bfloat16
F32 = jnp.float32
SELECT = 5


def iota(shape, dimension):
    return lax.broadcasted_iota(jnp.int32, shape, dimension)


def dot(a, b):
    return jnp.dot(a, b, preferred_element_type=F32)


def roll(x, shift):
    n = x.shape[1]
    return x if shift % n == 0 else pltpu.roll(x, (-shift) % n, 1)


def swap_rows(outer, inner):
    row, col = iota((128, 128), 0), iota((128, 128), 1)
    return jnp.where((row % outer) * inner + row // outer == col, 1.0, 0.0).astype(BF)


def pick_columns(zs):
    lane = iota((8, 128), 1)[0:1]
    group = lane >> 5
    z = jnp.where(group == 0, zs[0], jnp.where(group == 1, zs[1], jnp.where(group == 2, zs[2], zs[3])))
    return jnp.where(iota((CY * CZ, 128), 0) == (lane & 31) * CZ + z, 1.0, 0.0).astype(BF)


def with_neighbours(outer, inner):
    lane = iota(outer.shape, 1) & 127
    middle = jnp.where(
        lane < 64,
        jnp.where(lane < 32, roll(outer, 32), roll(inner, -32)),
        jnp.where(lane < 96, roll(inner, 32), roll(outer, -32)),
    )
    return jnp.where(lane < 64, outer, inner), middle, jnp.where(lane < 64, inner, outer)


def open_cells(mask):
    return jnp.concatenate([(1 - mask[x]).astype(F32) for x in range(8)], 0)


def bias_column(bias, shape):
    row = iota(shape, 0)
    column = jnp.zeros(shape, F32)
    for o in range(16):
        column = jnp.where(row == o, bias[o], column)
    return column


def select_kernel(out):
    out[...] = pick_columns((30, 31, 0, 1))


def pack_kernel(bias, select, one, weights):
    del select
    place = iota((16, 64), 1)
    column = bias_column(bias, (16, 64))
    high = column.astype(BF).astype(F32)
    middle = (column - high).astype(BF).astype(F32)
    terms = jnp.where(place == 0, high, jnp.where(place == 1, middle, jnp.where(place == 2, column - high - middle, 0.0)))
    for t in range(14):
        other = one[t + 14] if t < 13 else terms.astype(BF)
        weights[16 * t : 16 * t + 16] = jnp.concatenate([one[t], other], 1)


def rims_kernel(odd_ref, select, f, near, mask, first_out, second_out):
    lane = iota((144, 128), 1)
    opened = jnp.concatenate([open_cells(mask), jnp.zeros((8, CY * CZ), F32)], 0).astype(BF)
    own = dot(jnp.concatenate([f[...], opened], 0), select[...])
    other = dot(jnp.concatenate([near[...], opened], 0), select[...])
    last = jnp.where(lane < 64, own, roll(other, -64))
    early = jnp.where(lane < 64, roll(own, 64), other)
    odd = odd_ref[0] > 0
    first_out[...] = jnp.where(odd, early, last).astype(BF)
    second_out[...] = jnp.where(odd, last, early).astype(BF)


def place_features(base, f, field, rim):
    planes = dot(swap_rows(16, 8), f[...])
    rim[...] = dot(planes.astype(BF), pick_columns((0, 1, 30, 31)))
    for e in range(3):
        moved = roll(planes, e - 1).astype(BF)
        for x in range(8):
            field[pl.ds(192 * (x + 1) + 64 * e + base, 16)] = moved[16 * x : 16 * x + 16]


def place_filters(base, w, first, bias_one):
    def tap(t):
        block = w[16 * (t % 14) : 16 * (t % 14) + 16]
        return block[:, 0:64] if t < 14 else block[:, 64:128]

    blank = jnp.zeros((16, 192), BF)
    for b in range(3):
        taps = [tap(9 * a + 3 * b + e) for a in range(3) for e in range(3)]
        first[pl.ds(128 * b + base, 16)] = jnp.concatenate(taps + [blank], 1)
        first[pl.ds(128 * b + 64 + base, 16)] = jnp.concatenate([blank] + taps, 1)
    tail = w[16 * 13 : 16 * 14].astype(F32)
    total = tail[:, 64:65] + tail[:, 65:66] + tail[:, 66:67]
    bias_one[pl.ds(base, 16)] = jnp.broadcast_to(total, (16, 128))


def windows(x):
    return [(q, x + 1 - 2 * q) for q in range(4) if 0 <= x + 1 - 2 * q < 4]


def place_edges(me, chip, below, above, rims, edges):
    to_plane = swap_rows(16, 8)
    lane = iota((128, 128), 1)
    below, above = dot(to_plane, below), dot(to_plane, above)
    both = (jnp.where(lane < 64, below, roll(above, -64)), jnp.where(lane < 64, roll(below, 64), above))
    for core, outer in enumerate(both):
        k = 2 * chip + core
        base = pl.multiple_of((me ^ k) * 16, 16)
        for e, moved in enumerate(with_neighbours(outer, rims[k])):
            moved = moved.astype(BF)
            for x in range(8):
                for q, place in windows(x):
                    edges[pl.ds(192 * place + 64 * e + base, 16), 128 * q : 128 * q + 128] = moved[16 * x : 16 * x + 16]


def near_kernel(me_ref, bias, f0, f1, mask, two, field, rims, opened, open_rims, second, bias_two):
    field[0:192] = jnp.zeros((192, CY * CZ), BF)
    field[9 * 192 : 10 * 192] = jnp.zeros((192, CY * CZ), BF)
    cells = open_cells(mask)
    opened[...] = cells
    open_rims[...] = dot(cells.astype(BF), pick_columns((0, 1, 30, 31)))
    me = me_ref[0]
    for k, f in enumerate((f0, f1)):
        place_features(pl.multiple_of((me ^ k) * 16, 16), f, field, rims.at[k])
    blank = jnp.zeros((16, 64), BF)
    for e in range(3):
        for b in range(3):
            taps = [two[9 * a + 3 * b + e] for a in range(3)]
            row = 96 * e + 32 * b
            second[row : row + 16] = jnp.concatenate(taps + [blank], 1)
            second[row + 16 : row + 32] = jnp.concatenate([blank] + taps, 1)
    bias_two[...] = bias_column(bias, (16, 128))


def far_kernel(me_ref, f2, field_in, rims_in, field, rims):
    del field_in, rims_in
    place_features(pl.multiple_of((me_ref[0] ^ 2) * 16, 16), f2, field, rims.at[2])


def inside():
    lane = iota((8, CY * CZ), 1)[0:1]
    return jnp.where(lane >= CZ, 1.0, 0.0), jnp.where(lane < (CY - 1) * CZ, 1.0, 0.0)


def one_kernel(me_ref, f3, w0, w1, w2, w3, opened, below, above, field_in, rims_in, field, rims, hidden, first, bias_one, edges):
    del field_in, rims_in
    me = me_ref[0]
    for k, w in enumerate((w0, w1, w2, w3)):
        place_filters(pl.multiple_of((me ^ k) * 16, 16), w, first, bias_one)
    place_features(pl.multiple_of((me ^ 3) * 16, 16), f3, field, rims.at[3])

    edges[0:192, 0:128] = jnp.zeros((192, 128), BF)
    edges[576:768, 384:512] = jnp.zeros((192, 128), BF)
    place_edges(me, 0, below[0:128], above[0:128], rims, edges)

    after_first, before_last = inside()
    z = iota((8, CY * CZ), 1)[0:1] & 31
    settled = jnp.where((z > 0) & (z < CZ - 1), 1.0, 0.0)
    hidden[0:64] = jnp.zeros((64, CY * CZ), BF)
    hidden[9 * 64 : 10 * 64] = jnp.zeros((64, CY * CZ), BF)
    column = bias_one[:, 0:1]
    for q in range(4):
        sums = dot(first[...], field[384 * q : 384 * q + 768])
        total = roll(sums[0:128], -CZ) * after_first + sums[128:256] + roll(sums[256:384], CZ) * before_last
        for half in range(2):
            x = 2 * q + half
            value = jnp.maximum(total[64 * half : 64 * half + 64] + column, 0.0) * (opened[x : x + 1] * settled)
            hidden[64 * (x + 1) : 64 * (x + 2)] = value.astype(BF)


def two_kernel(me_ref, below, above, there, rims, open_rims, first, bias_one, second, bias_two, opened, hidden, edges_in,
               out_hbm, edges, edge, terms, sums, last, out, sems):
    del edges_in
    me = me_ref[0]
    has_before, has_after = inside()

    def settled(q):
        taken = dot(second[...], hidden[128 * q : 128 * q + 256])
        moved = [sum(roll(taken[96 * e + 32 * b : 96 * e + 32 * b + 32], e - 1) for e in range(3)) for b in range(3)]
        sums[32 * q : 32 * q + 32] = roll(moved[0], -CZ) * has_before + moved[1] + roll(moved[2], CZ) * has_after

    settled(0)
    place_edges(me, 1, there[0:128], there[128:256], rims, edges)
    lane = iota((8, 128), 1)
    open_halo = jnp.where(lane < 64, below[128:136].astype(F32), roll(above[128:136].astype(F32), -64))
    open_edge = with_neighbours(open_halo, open_rims[...])[1]
    settled(1)

    y = iota((8, 512), 1)[0:1] & 31
    after_first = jnp.where(y > 0, 1.0, 0.0)
    before_last = jnp.where(y < CY - 1, 1.0, 0.0)
    taken = dot(first[...], edges[...])
    total = roll(taken[0:128], -1) * after_first + taken[128:256] + roll(taken[256:384], 1) * before_last
    edge[0:64, 0:128] = jnp.zeros((64, 128), BF)
    edge[192:256, 384:512] = jnp.zeros((64, 128), BF)
    for half in range(2):
        opening = jnp.concatenate([open_edge[2 * q + half : 2 * q + half + 1] for q in range(4)], 1)
        value = jnp.maximum(total[64 * half : 64 * half + 64] + bias_one[:, 0:1], 0.0) * opening
        value = value.astype(BF)
        for k in range(4):
            for q, place in windows(2 * k + half):
                edge[64 * place : 64 * place + 64, 128 * q : 128 * q + 128] = value[:, 128 * k : 128 * k + 128]
    settled(2)

    taken = dot(second[...], edge[...])
    before, same, behind = [
        roll(taken[r : r + 32], -1) * after_first + taken[r + 32 : r + 64] + roll(taken[r + 64 : r + 96], 1) * before_last
        for r in (0, 96, 192)
    ]
    lane = iota((32, 512), 1) & 127
    total = jnp.where(lane < 64, before, behind)
    total += jnp.where(lane < 32, roll(same, 32), jnp.where(lane < 96, 0.0, roll(same, -32)))
    high = total.astype(BF)
    low = (total - high.astype(F32)).astype(BF)
    for q in range(4):
        terms[32 * q : 32 * q + 32] = high[:, 128 * q : 128 * q + 128]
        terms[128 + 32 * q : 160 + 32 * q] = low[:, 128 * q : 128 * q + 128]
    settled(3)

    cell = iota((8, CY * CZ), 1)[0:1]
    z = cell & 31
    row = jnp.where((z < 2) | (z >= 30), 32 * jnp.where(z < 2, z, z - 28) + (cell >> 5), -1)
    spread = dot(terms[...], jnp.where(iota((128, CY * CZ), 0) == row, 1.0, 0.0).astype(BF))
    to_channel = swap_rows(8, 16)
    copies = []
    for part, lanes in enumerate((slice(0, 512), slice(512, 1024))):
        for x in range(8):
            total = sums[16 * x : 16 * x + 16, lanes] + spread[16 * x : 16 * x + 16, lanes] + spread[128 + 16 * x : 144 + 16 * x, lanes]
            last[16 * x : 16 * x + 16, lanes] = (jnp.maximum(total + bias_two[:, 0:1], 0.0) * opened[x : x + 1, lanes]).astype(BF)
        out[:, lanes] = dot(to_channel, last[:, lanes]).astype(BF)
        copies.append(pltpu.make_async_copy(out.at[:, lanes], out_hbm.at[:, lanes], sems.at[part]))
        copies[-1].start()
    for copy in copies:
        copy.wait()


def cost(micros):
    return pl.CostEstimate(flops=int(micros * 1.15e9), bytes_accessed=int(micros * 3e6), transcendentals=0)


def one_row(features, solid_mask, weight_one, bias_one, weight_two, bias_two):
    columns = lax.axis_size("col")
    me = lax.axis_index("ch").astype(jnp.int32).reshape(1)

    def across(v, bit):
        return lax.ppermute(v, "ch", [(i, i ^ bit) for i in range(lax.axis_size("ch"))])

    def after(v, other):
        return lax.optimization_barrier((v, other))[0]

    def exchange(v, parity):
        route = []
        for c in range(parity, columns - 1, 2):
            route += [(c, c + 1), (c + 1, c)]
        return lax.ppermute(v, "col", route)

    smem = pl.BlockSpec(memory_space=pltpu.SMEM)
    vmem = pl.BlockSpec(memory_space=pltpu.VMEM)
    shape = jax.ShapeDtypeStruct

    cells = features.reshape(128, 1024)
    far = across(cells, 2)
    near = across(cells, 1)
    select = pl.pallas_call(
        select_kernel,
        out_shape=shape((1024, 128), BF),
        out_specs=vmem,
        compiler_params=pltpu.CompilerParams(vmem_limit_bytes=4 << 20),
        cost_estimate=cost(SELECT),
        name="select",
    )()
    weights = pl.pallas_call(
        pack_kernel,
        out_shape=shape((224, 128), BF),
        in_specs=[smem, vmem, vmem],
        out_specs=vmem,
        compiler_params=pltpu.CompilerParams(vmem_limit_bytes=8 << 20),
        cost_estimate=cost(0.5),
        name="pack",
    )(bias_one, select, weight_one.transpose(1, 0, 2))
    odd = (lax.axis_index("col") % 2).astype(jnp.int32)
    met_first, met_second = pl.pallas_call(
        rims_kernel,
        out_shape=[shape((144, 128), BF)] * 2,
        in_specs=[smem] + [vmem] * 4,
        out_specs=[vmem] * 2,
        compiler_params=pltpu.CompilerParams(vmem_limit_bytes=8 << 20),
        cost_estimate=cost(0.5),
        name="rims",
    )(odd.reshape(1), select, cells, near, solid_mask)
    met_second = exchange(met_second, 1)
    met_first = exchange(met_first, 0)
    weights_far, weights_near = across(weights, 2), across(weights, 1)

    field_shape, rims_shape = shape((1920, 1024), BF), shape((4, 128, 128), F32)
    field, rim_cells, opened, open_rims, second, bias_second = pl.pallas_call(
        near_kernel,
        out_shape=[field_shape, rims_shape, shape((8, 1024), F32), shape((8, 128), F32), shape((288, 256), BF), shape((16, 128), F32)],
        in_specs=[smem, smem] + [vmem] * 4,
        out_specs=[vmem] * 6,
        compiler_params=pltpu.CompilerParams(vmem_limit_bytes=16 << 20),
        cost_estimate=cost(0.1),
        name="near",
    )(me, bias_two, cells, near, solid_mask, weight_two.transpose(1, 0, 2))

    far = after(far, open_rims)
    cross = across(far, 1)
    field, rim_cells = pl.pallas_call(
        far_kernel,
        out_shape=[field_shape, rims_shape],
        in_specs=[smem] + [vmem] * 3,
        out_specs=[vmem] * 2,
        input_output_aliases={2: 0, 3: 1},
        compiler_params=pltpu.CompilerParams(vmem_limit_bytes=16 << 20),
        cost_estimate=cost(0.1),
        name="far",
    )(me, far, field, rim_cells)
    weights_far, rim_cells = lax.optimization_barrier((weights_far, rim_cells))
    weights_cross = across(weights_far, 1)

    met_first, met_second, rim_cells = lax.optimization_barrier((met_first, met_second, rim_cells))
    before = jnp.where(odd == 1, met_first, met_second)
    after_it = jnp.where(odd == 1, met_second, met_first)
    there = across(jnp.concatenate([before[:128], after_it[:128]], 0), 2)

    _, rim_cells, hidden, first, bias, edges = pl.pallas_call(
        one_kernel,
        out_shape=[field_shape, rims_shape, shape((640, 1024), BF), shape((384, 768), BF), shape((64, 128), F32), shape((768, 512), BF)],
        in_specs=[smem] + [vmem] * 10,
        out_specs=[vmem] * 6,
        input_output_aliases={9: 0, 10: 1},
        compiler_params=pltpu.CompilerParams(vmem_limit_bytes=24 << 20),
        cost_estimate=cost(4),
        name="one",
    )(me, cross, weights, weights_near, weights_far, weights_cross, opened, before, after_it, field, rim_cells)

    result, _ = pl.pallas_call(
        two_kernel,
        out_shape=[shape((128, 1024), BF), shape((768, 512), BF)],
        in_specs=[smem] + [vmem] * 12,
        out_specs=[pl.BlockSpec(memory_space=pltpu.HBM), vmem],
        input_output_aliases={12: 1},
        scratch_shapes=[
            pltpu.VMEM((256, 512), BF),
            pltpu.VMEM((256, 128), BF),
            pltpu.VMEM((128, 1024), F32),
            pltpu.VMEM((128, 1024), BF),
            pltpu.VMEM((128, 1024), BF),
            pltpu.SemaphoreType.DMA((2,)),
        ],
        compiler_params=pltpu.CompilerParams(vmem_limit_bytes=16 << 20),
        cost_estimate=cost(3),
        name="two",
    )(me, before, after_it, there, rim_cells, open_rims, first, bias, second, bias_second, opened, hidden, edges)
    return result.reshape(16, 8, 1, 1024)


def passed_along(block, axis, distance):
    devices = range(lax.axis_size(axis))
    route = [(i - distance, i) for i in devices if i - distance in devices]
    return lax.ppermute(block, axis, route)


def kernel_of(weight):
    outputs = weight.shape[0]
    inputs = weight.shape[2]
    return weight.reshape(outputs, 3, 3, 3, inputs).transpose(0, 4, 1, 2, 3)


def many_rows(features, solid_mask, weight_one, bias_one, weight_two, bias_two):
    cells = features.shape[3]
    columns = lax.axis_size("col")
    grid_z = min(8, columns)
    open_cells = (1 - solid_mask).astype(jnp.float32)

    def pad_columns(field):
        depth = field.shape[0]
        depth_x = field.shape[1]
        cube = field.reshape(depth, depth_x, CY, CZ)
        below = passed_along(cube[:, :, :, CZ - 1 :], "col", 1)
        above = passed_along(cube[:, :, :, :1], "col", -1)
        place = lax.axis_index("col") % grid_z
        below = jnp.where(place > 0, below, jnp.zeros_like(below))
        above = jnp.where(place < grid_z - 1, above, jnp.zeros_like(above))
        cube = jnp.concatenate([below, cube, above], axis=3)
        south = passed_along(cube[:, :, CY - 1 :, :], "col", grid_z)
        north = passed_along(cube[:, :, :1, :], "col", -grid_z)
        return jnp.concatenate([south, cube, north], axis=2)

    def pad_planes(framed):
        return jnp.pad(framed, ((0, 0), (1, 1), (0, 0), (0, 0)))

    def padded_inputs(field):
        whole = lax.all_gather(field, "ch", axis=0, tiled=True)
        framed = pad_columns(whole)
        return pad_planes(framed)

    def convolve(framed, weight):
        depth_x = framed.shape[1] - 2
        result = lax.conv_general_dilated(
            framed[None],
            kernel_of(weight),
            (1, 1, 1),
            "VALID",
            dimension_numbers=("NCDHW", "OIDHW", "NCDHW"),
            preferred_element_type=jnp.float32,
        )
        return result[0].reshape(weight.shape[0], depth_x, 1, cells)

    def finish(total, bias, opened):
        return (jnp.maximum(total + bias[:, None, None, None], 0.0) * opened[None]).astype(
            jnp.bfloat16
        )

    hidden = finish(convolve(padded_inputs(features), weight_one), bias_one, open_cells)
    total = convolve(padded_inputs(hidden), weight_two)
    return finish(total, bias_two, open_cells)


def on_device(*arguments):
    columns = lax.axis_size("col")
    return one_row(*arguments) if columns <= 8 and columns % 2 == 0 else many_rows(*arguments)


def solution(mesh):
    in_specs = (
        P("ch", None, "col", None),
        P(None, "col", None),
        P("ch", None, None),
        P("ch"),
        P("ch", None, None),
        P("ch"),
    )
    out_specs = P("ch", None, "col", None)
    return jax.shard_map(
        on_device, mesh=mesh, in_specs=in_specs, out_specs=out_specs, check_vma=False
    )
```

```python
import jax
import jax.numpy as jnp
from jax import lax
from jax.experimental import pallas as pl
from jax.experimental.pallas import tpu as pltpu
from jax.sharding import PartitionSpec as P

CY = 32
CZ = 32
BF = jnp.bfloat16
F32 = jnp.float32
SELECT = 5


def iota(shape, dimension):
    return lax.broadcasted_iota(jnp.int32, shape, dimension)


def dot(a, b):
    return jnp.dot(a, b, preferred_element_type=F32)


def roll(x, shift):
    n = x.shape[1]
    return x if shift % n == 0 else pltpu.roll(x, (-shift) % n, 1)


def swap_rows(outer, inner):
    row, col = iota((128, 128), 0), iota((128, 128), 1)
    return jnp.where((row % outer) * inner + row // outer == col, 1.0, 0.0).astype(BF)


def pick_columns(zs):
    lane = iota((8, 128), 1)[0:1]
    group = lane >> 5
    z = jnp.where(group == 0, zs[0], jnp.where(group == 1, zs[1], jnp.where(group == 2, zs[2], zs[3])))
    return jnp.where(iota((CY * CZ, 128), 0) == (lane & 31) * CZ + z, 1.0, 0.0).astype(BF)


def with_neighbours(outer, inner):
    lane = iota(outer.shape, 1) & 127
    middle = jnp.where(
        lane < 64,
        jnp.where(lane < 32, roll(outer, 32), roll(inner, -32)),
        jnp.where(lane < 96, roll(inner, 32), roll(outer, -32)),
    )
    return jnp.where(lane < 64, outer, inner), middle, jnp.where(lane < 64, inner, outer)


def open_cells(mask):
    return jnp.concatenate([(1 - mask[x]).astype(F32) for x in range(8)], 0)


def bias_column(bias, shape):
    diagonal = jnp.where(iota((16, 16), 0) == iota((16, 16), 1), bias[...], 0.0)
    return jnp.broadcast_to(jnp.sum(diagonal, 1, keepdims=True), shape)


def select_kernel(out):
    out[...] = pick_columns((30, 31, 0, 1))


def pack_kernel(bias, select, one, weights):
    del select
    place = iota((16, 64), 1)
    column = bias_column(bias, (16, 64))
    high = column.astype(BF).astype(F32)
    middle = (column - high).astype(BF).astype(F32)
    terms = jnp.where(place == 0, high, jnp.where(place == 1, middle, jnp.where(place == 2, column - high - middle, 0.0)))
    for t in range(14):
        other = one[t + 14] if t < 13 else terms.astype(BF)
        weights[16 * t : 16 * t + 16] = jnp.concatenate([one[t], other], 1)


def rims_kernel(select, f, mask, rims):
    opened = jnp.concatenate([open_cells(mask), jnp.zeros((8, CY * CZ), F32)], 0).astype(BF)
    own = dot(jnp.concatenate([f[...], opened], 0), select[...])
    rims[0:144] = own.astype(BF)
    rims[144:288] = roll(own, 64).astype(BF)


def place_features(base, f, field, rim):
    planes = dot(swap_rows(16, 8), f[...])
    rim[...] = dot(planes.astype(BF), pick_columns((0, 1, 30, 31)))
    for e in range(3):
        moved = roll(planes, e - 1).astype(BF)
        for x in range(8):
            field[pl.ds(192 * (x + 1) + 64 * e + base, 16)] = moved[16 * x : 16 * x + 16]


def place_filters(base, w, first, bias_one):
    def tap(t):
        block = w[16 * (t % 14) : 16 * (t % 14) + 16]
        return block[:, 0:64] if t < 14 else block[:, 64:128]

    blank = jnp.zeros((16, 192), BF)
    for b in range(3):
        taps = [tap(9 * a + 3 * b + e) for a in range(3) for e in range(3)]
        first[pl.ds(128 * b + base, 16)] = jnp.concatenate(taps + [blank], 1)
        first[pl.ds(128 * b + 64 + base, 16)] = jnp.concatenate([blank] + taps, 1)
    tail = w[16 * 13 : 16 * 14].astype(F32)
    total = tail[:, 64:65] + tail[:, 65:66] + tail[:, 66:67]
    bias_one[pl.ds(base, 16)] = jnp.broadcast_to(total, (16, 128))


def windows(x):
    return [(q, x + 1 - 2 * q) for q in range(4) if 0 <= x + 1 - 2 * q < 4]


def place_edges(me, chip, below, above, rims, edges):
    to_plane = swap_rows(16, 8)
    lane = iota((128, 128), 1)
    below, above = dot(to_plane, below), dot(to_plane, above)
    both = (jnp.where(lane < 64, below, roll(above, -64)), jnp.where(lane < 64, roll(below, 64), above))
    for core, outer in enumerate(both):
        k = 2 * chip + core
        base = pl.multiple_of((me ^ k) * 16, 16)
        for e, moved in enumerate(with_neighbours(outer, rims[k])):
            moved = moved.astype(BF)
            for x in range(8):
                for q, place in windows(x):
                    edges[pl.ds(192 * place + 64 * e + base, 16), 128 * q : 128 * q + 128] = moved[16 * x : 16 * x + 16]


def near_kernel(bias, f0, f1, mask, two, field, rims, opened, open_rims, second, bias_two):
    field[0:192] = jnp.zeros((192, CY * CZ), BF)
    field[9 * 192 : 10 * 192] = jnp.zeros((192, CY * CZ), BF)
    cells = open_cells(mask)
    opened[...] = cells
    open_rims[...] = dot(cells.astype(BF), pick_columns((0, 1, 30, 31)))
    me = lax.axis_index("ch")
    for k, f in enumerate((f0, f1)):
        place_features(pl.multiple_of((me ^ k) * 16, 16), f, field, rims.at[k])
    blank = jnp.zeros((16, 64), BF)
    for e in range(3):
        for b in range(3):
            taps = [two[9 * a + 3 * b + e] for a in range(3)]
            row = 96 * e + 32 * b
            second[row : row + 16] = jnp.concatenate(taps + [blank], 1)
            second[row + 16 : row + 32] = jnp.concatenate([blank] + taps, 1)
    bias_two[...] = bias_column(bias, (16, 128))


def far_kernel(f2, field_in, rims_in, field, rims):
    del field_in, rims_in
    place_features(pl.multiple_of((lax.axis_index("ch") ^ 2) * 16, 16), f2, field, rims.at[2])


def inside():
    lane = iota((8, CY * CZ), 1)[0:1]
    return jnp.where(lane >= CZ, 1.0, 0.0), jnp.where(lane < (CY - 1) * CZ, 1.0, 0.0)


def one_kernel(f3, w0, w1, w2, w3, opened, below, above, field_in, rims_in, field, rims, hidden, first, bias_one, edges):
    del field_in, rims_in
    me = lax.axis_index("ch")
    for k, w in enumerate((w0, w1, w2, w3)):
        place_filters(pl.multiple_of((me ^ k) * 16, 16), w, first, bias_one)
    place_features(pl.multiple_of((me ^ 3) * 16, 16), f3, field, rims.at[3])

    edges[0:192, 0:128] = jnp.zeros((192, 128), BF)
    edges[576:768, 384:512] = jnp.zeros((192, 128), BF)
    place_edges(me, 0, below[0:128], above[0:128], rims, edges)

    after_first, before_last = inside()
    z = iota((8, CY * CZ), 1)[0:1] & 31
    settled = jnp.where((z > 0) & (z < CZ - 1), 1.0, 0.0)
    hidden[0:64] = jnp.zeros((64, CY * CZ), BF)
    hidden[9 * 64 : 10 * 64] = jnp.zeros((64, CY * CZ), BF)
    column = bias_one[:, 0:1]
    for q in range(4):
        sums = dot(first[...], field[384 * q : 384 * q + 768])
        total = roll(sums[0:128], -CZ) * after_first + sums[128:256] + roll(sums[256:384], CZ) * before_last
        for half in range(2):
            x = 2 * q + half
            value = jnp.maximum(total[64 * half : 64 * half + 64] + column, 0.0) * (opened[x : x + 1] * settled)
            hidden[64 * (x + 1) : 64 * (x + 2)] = value.astype(BF)


def two_kernel(below, above, there, rims, open_rims, first, bias_one, second, bias_two, opened, hidden, edges_in,
               out_hbm, edges, edge, terms, sums, last, out, sems):
    del edges_in
    me = lax.axis_index("ch")
    has_before, has_after = inside()

    def settled(q):
        taken = dot(second[...], hidden[128 * q : 128 * q + 256])
        moved = [sum(roll(taken[96 * e + 32 * b : 96 * e + 32 * b + 32], e - 1) for e in range(3)) for b in range(3)]
        sums[32 * q : 32 * q + 32] = roll(moved[0], -CZ) * has_before + moved[1] + roll(moved[2], CZ) * has_after

    settled(0)
    place_edges(me, 1, there[0:128], there[128:256], rims, edges)
    lane = iota((8, 128), 1)
    open_halo = jnp.where(lane < 64, below[128:136].astype(F32), roll(above[128:136].astype(F32), -64))
    open_edge = with_neighbours(open_halo, open_rims[...])[1]
    settled(1)

    y = iota((8, 512), 1)[0:1] & 31
    after_first = jnp.where(y > 0, 1.0, 0.0)
    before_last = jnp.where(y < CY - 1, 1.0, 0.0)
    taken = dot(first[...], edges[...])
    total = roll(taken[0:128], -1) * after_first + taken[128:256] + roll(taken[256:384], 1) * before_last
    edge[0:64, 0:128] = jnp.zeros((64, 128), BF)
    edge[192:256, 384:512] = jnp.zeros((64, 128), BF)
    for half in range(2):
        opening = jnp.concatenate([open_edge[2 * q + half : 2 * q + half + 1] for q in range(4)], 1)
        value = jnp.maximum(total[64 * half : 64 * half + 64] + bias_one[:, 0:1], 0.0) * opening
        value = value.astype(BF)
        for k in range(4):
            for q, place in windows(2 * k + half):
                edge[64 * place : 64 * place + 64, 128 * q : 128 * q + 128] = value[:, 128 * k : 128 * k + 128]
    settled(2)

    taken = dot(second[...], edge[...])
    before, same, behind = [
        roll(taken[r : r + 32], -1) * after_first + taken[r + 32 : r + 64] + roll(taken[r + 64 : r + 96], 1) * before_last
        for r in (0, 96, 192)
    ]
    lane = iota((32, 512), 1) & 127
    total = jnp.where(lane < 64, before, behind)
    total += jnp.where(lane < 32, roll(same, 32), jnp.where(lane < 96, 0.0, roll(same, -32)))
    high = total.astype(BF)
    low = (total - high.astype(F32)).astype(BF)
    for q in range(4):
        terms[32 * q : 32 * q + 32] = high[:, 128 * q : 128 * q + 128]
        terms[128 + 32 * q : 160 + 32 * q] = low[:, 128 * q : 128 * q + 128]
    settled(3)

    cell = iota((8, CY * CZ), 1)[0:1]
    z = cell & 31
    row = jnp.where((z < 2) | (z >= 30), 32 * jnp.where(z < 2, z, z - 28) + (cell >> 5), -1)
    spread = dot(terms[...], jnp.where(iota((128, CY * CZ), 0) == row, 1.0, 0.0).astype(BF))
    to_channel = swap_rows(8, 16)
    copies = []
    for part, lanes in enumerate((slice(0, 512), slice(512, 1024))):
        for x in range(8):
            total = sums[16 * x : 16 * x + 16, lanes] + spread[16 * x : 16 * x + 16, lanes] + spread[128 + 16 * x : 144 + 16 * x, lanes]
            last[16 * x : 16 * x + 16, lanes] = (jnp.maximum(total + bias_two[:, 0:1], 0.0) * opened[x : x + 1, lanes]).astype(BF)
        out[:, lanes] = dot(to_channel, last[:, lanes]).astype(BF)
        copies.append(pltpu.make_async_copy(out.at[:, lanes], out_hbm.at[:, lanes], sems.at[part]))
        copies[-1].start()
    for copy in copies:
        copy.wait()


def cost(micros):
    return pl.CostEstimate(flops=int(micros * 1.15e9), bytes_accessed=int(micros * 3e6), transcendentals=0)


def one_row(features, solid_mask, weight_one, bias_one, weight_two, bias_two):
    columns = lax.axis_size("col")

    def across(v, bit):
        return lax.ppermute(v, "ch", [(i, i ^ bit) for i in range(lax.axis_size("ch"))])

    def after(v, other):
        return lax.optimization_barrier((v, other))[0]

    def exchange(v, parity):
        route = []
        for c in range(parity, columns - 1, 2):
            route += [(c, c + 1), (c + 1, c)]
        return lax.ppermute(v, "col", route)

    vmem = pl.BlockSpec(memory_space=pltpu.VMEM)
    shape = jax.ShapeDtypeStruct

    cells = features.reshape(128, 1024)
    far = across(cells, 2)
    select = pl.pallas_call(
        select_kernel,
        out_shape=shape((1024, 128), BF),
        out_specs=vmem,
        compiler_params=pltpu.CompilerParams(vmem_limit_bytes=4 << 20),
        cost_estimate=cost(SELECT),
        name="select",
    )()
    weights = pl.pallas_call(
        pack_kernel,
        out_shape=shape((224, 128), BF),
        in_specs=[vmem, vmem, vmem],
        out_specs=vmem,
        compiler_params=pltpu.CompilerParams(vmem_limit_bytes=8 << 20),
        cost_estimate=cost(0.5),
        name="pack",
    )(bias_one.reshape(1, 16), select, weight_one.transpose(1, 0, 2))
    rims = pl.pallas_call(
        rims_kernel,
        out_shape=shape((288, 128), BF),
        in_specs=[vmem] * 3,
        out_specs=vmem,
        compiler_params=pltpu.CompilerParams(vmem_limit_bytes=8 << 20),
        cost_estimate=cost(0.5),
        name="rims",
    )(select, cells, solid_mask)
    rims_near = across(rims, 1)
    near = across(after(cells, rims), 1)

    odd = lax.axis_index("col") % 2 == 1
    low = lax.broadcasted_iota(jnp.int32, (144, 128), 1) < 64
    last = jnp.where(low, rims[:144], rims_near[144:])
    early = jnp.where(low, rims[144:], rims_near[:144])
    met_second = exchange(jnp.where(odd, last, early), 1)
    met_first = exchange(jnp.where(odd, early, last), 0)
    weights_far, weights_near = across(weights, 2), across(weights, 1)

    field_shape, rims_shape = shape((1920, 1024), BF), shape((4, 128, 128), F32)
    field, rim_cells, opened, open_rims, second, bias_second = pl.pallas_call(
        near_kernel,
        out_shape=[field_shape, rims_shape, shape((8, 1024), F32), shape((8, 128), F32), shape((288, 256), BF), shape((16, 128), F32)],
        in_specs=[vmem] * 5,
        out_specs=[vmem] * 6,
        compiler_params=pltpu.CompilerParams(vmem_limit_bytes=16 << 20),
        cost_estimate=cost(0.1),
        name="near",
    )(bias_two.reshape(1, 16), cells, near, solid_mask, weight_two.transpose(1, 0, 2))

    far = after(far, open_rims)
    cross = across(far, 1)
    field, rim_cells = pl.pallas_call(
        far_kernel,
        out_shape=[field_shape, rims_shape],
        in_specs=[vmem] * 3,
        out_specs=[vmem] * 2,
        input_output_aliases={1: 0, 2: 1},
        compiler_params=pltpu.CompilerParams(vmem_limit_bytes=16 << 20),
        cost_estimate=cost(0.1),
        name="far",
    )(far, field, rim_cells)
    weights_far, rim_cells = lax.optimization_barrier((weights_far, rim_cells))
    weights_cross = across(weights_far, 1)

    met_second, met_first, rim_cells = lax.optimization_barrier((met_second, met_first, rim_cells))
    before = jnp.where(odd, met_first, met_second)
    after_it = jnp.where(odd, met_second, met_first)
    there = across(jnp.concatenate([before[:128], after_it[:128]], 0), 2)

    _, rim_cells, hidden, first, bias, edges = pl.pallas_call(
        one_kernel,
        out_shape=[field_shape, rims_shape, shape((640, 1024), BF), shape((384, 768), BF), shape((64, 128), F32), shape((768, 512), BF)],
        in_specs=[vmem] * 10,
        out_specs=[vmem] * 6,
        input_output_aliases={8: 0, 9: 1},
        compiler_params=pltpu.CompilerParams(vmem_limit_bytes=24 << 20),
        cost_estimate=cost(4),
        name="one",
    )(cross, weights, weights_near, weights_far, weights_cross, opened, before, after_it, field, rim_cells)

    result, _ = pl.pallas_call(
        two_kernel,
        out_shape=[shape((128, 1024), BF), shape((768, 512), BF)],
        in_specs=[vmem] * 12,
        out_specs=[pl.BlockSpec(memory_space=pltpu.HBM), vmem],
        input_output_aliases={11: 1},
        scratch_shapes=[
            pltpu.VMEM((256, 512), BF),
            pltpu.VMEM((256, 128), BF),
            pltpu.VMEM((128, 1024), F32),
            pltpu.VMEM((128, 1024), BF),
            pltpu.VMEM((128, 1024), BF),
            pltpu.SemaphoreType.DMA((2,)),
        ],
        compiler_params=pltpu.CompilerParams(vmem_limit_bytes=16 << 20),
        cost_estimate=cost(3),
        name="two",
    )(before, after_it, there, rim_cells, open_rims, first, bias, second, bias_second, opened, hidden, edges)
    return result.reshape(16, 8, 1, 1024)


def passed_along(block, axis, distance):
    devices = range(lax.axis_size(axis))
    route = [(i - distance, i) for i in devices if i - distance in devices]
    return lax.ppermute(block, axis, route)


def kernel_of(weight):
    outputs = weight.shape[0]
    inputs = weight.shape[2]
    return weight.reshape(outputs, 3, 3, 3, inputs).transpose(0, 4, 1, 2, 3)


def many_rows(features, solid_mask, weight_one, bias_one, weight_two, bias_two):
    cells = features.shape[3]
    columns = lax.axis_size("col")
    grid_z = min(8, columns)
    open_cells = (1 - solid_mask).astype(jnp.float32)

    def pad_columns(field):
        depth = field.shape[0]
        depth_x = field.shape[1]
        cube = field.reshape(depth, depth_x, CY, CZ)
        below = passed_along(cube[:, :, :, CZ - 1 :], "col", 1)
        above = passed_along(cube[:, :, :, :1], "col", -1)
        place = lax.axis_index("col") % grid_z
        below = jnp.where(place > 0, below, jnp.zeros_like(below))
        above = jnp.where(place < grid_z - 1, above, jnp.zeros_like(above))
        cube = jnp.concatenate([below, cube, above], axis=3)
        south = passed_along(cube[:, :, CY - 1 :, :], "col", grid_z)
        north = passed_along(cube[:, :, :1, :], "col", -grid_z)
        return jnp.concatenate([south, cube, north], axis=2)

    def pad_planes(framed):
        return jnp.pad(framed, ((0, 0), (1, 1), (0, 0), (0, 0)))

    def padded_inputs(field):
        whole = lax.all_gather(field, "ch", axis=0, tiled=True)
        framed = pad_columns(whole)
        return pad_planes(framed)

    def convolve(framed, weight):
        depth_x = framed.shape[1] - 2
        result = lax.conv_general_dilated(
            framed[None],
            kernel_of(weight),
            (1, 1, 1),
            "VALID",
            dimension_numbers=("NCDHW", "OIDHW", "NCDHW"),
            preferred_element_type=jnp.float32,
        )
        return result[0].reshape(weight.shape[0], depth_x, 1, cells)

    def finish(total, bias, opened):
        return (jnp.maximum(total + bias[:, None, None, None], 0.0) * opened[None]).astype(
            jnp.bfloat16
        )

    hidden = finish(convolve(padded_inputs(features), weight_one), bias_one, open_cells)
    total = convolve(padded_inputs(hidden), weight_two)
    return finish(total, bias_two, open_cells)


def on_device(*arguments):
    columns = lax.axis_size("col")
    return one_row(*arguments) if columns <= 8 and columns % 2 == 0 else many_rows(*arguments)


def solution(mesh):
    in_specs = (
        P("ch", None, "col", None),
        P(None, "col", None),
        P("ch", None, None),
        P("ch"),
        P("ch", None, None),
        P("ch"),
    )
    out_specs = P("ch", None, "col", None)
    return jax.shard_map(
        on_device, mesh=mesh, in_specs=in_specs, out_specs=out_specs, check_vma=False
    )
```

```python
import jax
import jax.numpy as jnp
from jax import lax
from jax.experimental import pallas as pl
from jax.experimental.pallas import tpu as pltpu
from jax.sharding import PartitionSpec as P

CY = 32
CZ = 32
BF = jnp.bfloat16
F32 = jnp.float32
SELECT = 5


def iota(shape, dimension):
    return lax.broadcasted_iota(jnp.int32, shape, dimension)


def dot(a, b):
    return jnp.dot(a, b, preferred_element_type=F32)


def roll(x, shift):
    n = x.shape[1]
    return x if shift % n == 0 else pltpu.roll(x, (-shift) % n, 1)


def swap_rows(outer, inner):
    row, col = iota((128, 128), 0), iota((128, 128), 1)
    return jnp.where((row % outer) * inner + row // outer == col, 1.0, 0.0).astype(BF)


def pick_columns(zs):
    lane = iota((8, 128), 1)[0:1]
    group = lane >> 5
    z = jnp.where(group == 0, zs[0], jnp.where(group == 1, zs[1], jnp.where(group == 2, zs[2], zs[3])))
    return jnp.where(iota((CY * CZ, 128), 0) == (lane & 31) * CZ + z, 1.0, 0.0).astype(BF)


def with_neighbours(outer, inner):
    lane = iota(outer.shape, 1) & 127
    middle = jnp.where(
        lane < 64,
        jnp.where(lane < 32, roll(outer, 32), roll(inner, -32)),
        jnp.where(lane < 96, roll(inner, 32), roll(outer, -32)),
    )
    return jnp.where(lane < 64, outer, inner), middle, jnp.where(lane < 64, inner, outer)


def open_cells(mask):
    return jnp.concatenate([(1 - mask[x]).astype(F32) for x in range(8)], 0)


def bias_column(bias, shape):
    diagonal = jnp.where(iota((16, 16), 0) == iota((16, 16), 1), bias[...], 0.0)
    return jnp.broadcast_to(jnp.sum(diagonal, 1, keepdims=True), shape)


def select_kernel(out):
    out[...] = pick_columns((30, 31, 0, 1))


def pack_kernel(bias, select, one, weights):
    del select
    place = iota((16, 64), 1)
    column = bias_column(bias, (16, 64))
    high = column.astype(BF).astype(F32)
    middle = (column - high).astype(BF).astype(F32)
    terms = jnp.where(place == 0, high, jnp.where(place == 1, middle, jnp.where(place == 2, column - high - middle, 0.0)))
    for t in range(14):
        other = one[t + 14] if t < 13 else terms.astype(BF)
        weights[16 * t : 16 * t + 16] = jnp.concatenate([one[t], other], 1)


def rims_kernel(select, f, mask, rims):
    opened = jnp.concatenate([open_cells(mask), jnp.zeros((8, CY * CZ), F32)], 0).astype(BF)
    own = dot(jnp.concatenate([f[...], opened], 0), select[...])
    rims[0:144] = own.astype(BF)
    rims[144:288] = roll(own, 64).astype(BF)


def place_features(base, f, field, rim):
    planes = dot(swap_rows(16, 8), f[...])
    rim[...] = dot(planes.astype(BF), pick_columns((0, 1, 30, 31)))
    for e in range(3):
        moved = roll(planes, e - 1).astype(BF)
        for x in range(8):
            field[pl.ds(192 * (x + 1) + 64 * e + base, 16)] = moved[16 * x : 16 * x + 16]


def place_filters(base, w, first, bias_one):
    def tap(t):
        block = w[16 * (t % 14) : 16 * (t % 14) + 16]
        return block[:, 0:64] if t < 14 else block[:, 64:128]

    blank = jnp.zeros((16, 192), BF)
    for b in range(3):
        taps = [tap(9 * a + 3 * b + e) for a in range(3) for e in range(3)]
        first[pl.ds(128 * b + base, 16)] = jnp.concatenate(taps + [blank], 1)
        first[pl.ds(128 * b + 64 + base, 16)] = jnp.concatenate([blank] + taps, 1)
    tail = w[16 * 13 : 16 * 14].astype(F32)
    total = tail[:, 64:65] + tail[:, 65:66] + tail[:, 66:67]
    bias_one[pl.ds(base, 16)] = jnp.broadcast_to(total, (16, 128))


def windows(x):
    return [(q, x + 1 - 2 * q) for q in range(4) if 0 <= x + 1 - 2 * q < 4]


def place_edges(me, chip, below, above, rims, edges):
    to_plane = swap_rows(16, 8)
    lane = iota((128, 128), 1)
    below, above = dot(to_plane, below), dot(to_plane, above)
    both = (jnp.where(lane < 64, below, roll(above, -64)), jnp.where(lane < 64, roll(below, 64), above))
    for core, outer in enumerate(both):
        k = 2 * chip + core
        base = pl.multiple_of((me ^ k) * 16, 16)
        for e, moved in enumerate(with_neighbours(outer, rims[k])):
            moved = moved.astype(BF)
            for x in range(8):
                for q, place in windows(x):
                    edges[pl.ds(192 * place + 64 * e + base, 16), 128 * q : 128 * q + 128] = moved[16 * x : 16 * x + 16]


def near_kernel(bias, f0, f1, mask, two, field, rims, opened, open_rims, second, bias_two):
    field[0:192] = jnp.zeros((192, CY * CZ), BF)
    field[9 * 192 : 10 * 192] = jnp.zeros((192, CY * CZ), BF)
    cells = open_cells(mask)
    opened[...] = cells
    open_rims[...] = dot(cells.astype(BF), pick_columns((0, 1, 30, 31)))
    me = lax.axis_index("ch")
    for k, f in enumerate((f0, f1)):
        place_features(pl.multiple_of((me ^ k) * 16, 16), f, field, rims.at[k])
    blank = jnp.zeros((16, 64), BF)
    for e in range(3):
        for b in range(3):
            taps = [two[9 * a + 3 * b + e] for a in range(3)]
            row = 96 * e + 32 * b
            second[row : row + 16] = jnp.concatenate(taps + [blank], 1)
            second[row + 16 : row + 32] = jnp.concatenate([blank] + taps, 1)
    bias_two[...] = bias_column(bias, (16, 128))


def far_kernel(f2, field_in, rims_in, field, rims):
    del field_in, rims_in
    place_features(pl.multiple_of((lax.axis_index("ch") ^ 2) * 16, 16), f2, field, rims.at[2])


def inside():
    lane = iota((8, CY * CZ), 1)[0:1]
    return jnp.where(lane >= CZ, 1.0, 0.0), jnp.where(lane < (CY - 1) * CZ, 1.0, 0.0)


def one_kernel(f3, w0, w1, w2, w3, opened, below, above, field_in, rims_in, field, rims, hidden, first, bias_one, edges):
    del field_in, rims_in
    me = lax.axis_index("ch")
    for k, w in enumerate((w0, w1, w2, w3)):
        place_filters(pl.multiple_of((me ^ k) * 16, 16), w, first, bias_one)
    place_features(pl.multiple_of((me ^ 3) * 16, 16), f3, field, rims.at[3])

    edges[0:192, 0:128] = jnp.zeros((192, 128), BF)
    edges[576:768, 384:512] = jnp.zeros((192, 128), BF)
    place_edges(me, 0, below[0:128], above[0:128], rims, edges)

    after_first, before_last = inside()
    z = iota((8, CY * CZ), 1)[0:1] & 31
    settled = jnp.where((z > 0) & (z < CZ - 1), 1.0, 0.0)
    hidden[0:64] = jnp.zeros((64, CY * CZ), BF)
    hidden[9 * 64 : 10 * 64] = jnp.zeros((64, CY * CZ), BF)
    column = bias_one[:, 0:1]
    for q in range(4):
        sums = dot(first[...], field[384 * q : 384 * q + 768])
        total = roll(sums[0:128], -CZ) * after_first + sums[128:256] + roll(sums[256:384], CZ) * before_last
        for half in range(2):
            x = 2 * q + half
            value = jnp.maximum(total[64 * half : 64 * half + 64] + column, 0.0) * (opened[x : x + 1] * settled)
            hidden[64 * (x + 1) : 64 * (x + 2)] = value.astype(BF)


def two_kernel(below, above, there, rims, open_rims, first, bias_one, second, bias_two, opened, hidden, edges_in,
               out_hbm, edges, edge, terms, sums, last, out, sems):
    del edges_in
    me = lax.axis_index("ch")
    has_before, has_after = inside()

    def settled(q):
        taken = dot(second[...], hidden[128 * q : 128 * q + 256])
        moved = [sum(roll(taken[96 * e + 32 * b : 96 * e + 32 * b + 32], e - 1) for e in range(3)) for b in range(3)]
        sums[32 * q : 32 * q + 32] = roll(moved[0], -CZ) * has_before + moved[1] + roll(moved[2], CZ) * has_after

    settled(0)
    place_edges(me, 1, there[0:128], there[128:256], rims, edges)
    lane = iota((8, 128), 1)
    open_halo = jnp.where(lane < 64, below[128:136].astype(F32), roll(above[128:136].astype(F32), -64))
    open_edge = with_neighbours(open_halo, open_rims[...])[1]
    settled(1)

    y = iota((8, 512), 1)[0:1] & 31
    after_first = jnp.where(y > 0, 1.0, 0.0)
    before_last = jnp.where(y < CY - 1, 1.0, 0.0)
    taken = dot(first[...], edges[...])
    total = roll(taken[0:128], -1) * after_first + taken[128:256] + roll(taken[256:384], 1) * before_last
    edge[0:64, 0:128] = jnp.zeros((64, 128), BF)
    edge[192:256, 384:512] = jnp.zeros((64, 128), BF)
    for half in range(2):
        opening = jnp.concatenate([open_edge[2 * q + half : 2 * q + half + 1] for q in range(4)], 1)
        value = jnp.maximum(total[64 * half : 64 * half + 64] + bias_one[:, 0:1], 0.0) * opening
        value = value.astype(BF)
        for k in range(4):
            for q, place in windows(2 * k + half):
                edge[64 * place : 64 * place + 64, 128 * q : 128 * q + 128] = value[:, 128 * k : 128 * k + 128]
    settled(2)

    taken = dot(second[...], edge[...])
    before, same, behind = [
        roll(taken[r : r + 32], -1) * after_first + taken[r + 32 : r + 64] + roll(taken[r + 64 : r + 96], 1) * before_last
        for r in (0, 96, 192)
    ]
    lane = iota((32, 512), 1) & 127
    total = jnp.where(lane < 64, before, behind)
    total += jnp.where(lane < 32, roll(same, 32), jnp.where(lane < 96, 0.0, roll(same, -32)))
    high = total.astype(BF)
    low = (total - high.astype(F32)).astype(BF)
    for q in range(4):
        terms[32 * q : 32 * q + 32] = high[:, 128 * q : 128 * q + 128]
        terms[128 + 32 * q : 160 + 32 * q] = low[:, 128 * q : 128 * q + 128]
    settled(3)

    cell = iota((8, CY * CZ), 1)[0:1]
    z = cell & 31
    row = jnp.where((z < 2) | (z >= 30), 32 * jnp.where(z < 2, z, z - 28) + (cell >> 5), -1)
    spread = dot(terms[...], jnp.where(iota((128, CY * CZ), 0) == row, 1.0, 0.0).astype(BF))
    to_channel = swap_rows(8, 16)
    copies = []
    for part, lanes in enumerate((slice(0, 512), slice(512, 1024))):
        for x in range(8):
            total = sums[16 * x : 16 * x + 16, lanes] + spread[16 * x : 16 * x + 16, lanes] + spread[128 + 16 * x : 144 + 16 * x, lanes]
            last[16 * x : 16 * x + 16, lanes] = (jnp.maximum(total + bias_two[:, 0:1], 0.0) * opened[x : x + 1, lanes]).astype(BF)
        out[:, lanes] = dot(to_channel, last[:, lanes]).astype(BF)
        copies.append(pltpu.make_async_copy(out.at[:, lanes], out_hbm.at[:, lanes], sems.at[part]))
        copies[-1].start()
    for copy in copies:
        copy.wait()


def cost(micros):
    return pl.CostEstimate(flops=int(micros * 1.15e9), bytes_accessed=int(micros * 3e6), transcendentals=0)


def one_row(features, solid_mask, weight_one, bias_one, weight_two, bias_two):
    columns = lax.axis_size("col")

    def across(v, bit):
        return lax.ppermute(v, "ch", [(i, i ^ bit) for i in range(lax.axis_size("ch"))])

    def after(v, other):
        return lax.optimization_barrier((v, other))[0]

    def exchange(v, parity):
        route = []
        for c in range(parity, columns - 1, 2):
            route += [(c, c + 1), (c + 1, c)]
        return lax.ppermute(v, "col", route)

    vmem = pl.BlockSpec(memory_space=pltpu.VMEM)
    shape = jax.ShapeDtypeStruct

    cells = features.reshape(128, 1024)
    far = across(cells, 2)
    select = pl.pallas_call(
        select_kernel,
        out_shape=shape((1024, 128), BF),
        out_specs=vmem,
        compiler_params=pltpu.CompilerParams(vmem_limit_bytes=4 << 20),
        cost_estimate=cost(SELECT),
        name="select",
    )()
    weights = pl.pallas_call(
        pack_kernel,
        out_shape=shape((224, 128), BF),
        in_specs=[vmem, vmem, vmem],
        out_specs=vmem,
        compiler_params=pltpu.CompilerParams(vmem_limit_bytes=8 << 20),
        cost_estimate=cost(0.5),
        name="pack",
    )(bias_one.reshape(1, 16), select, weight_one.transpose(1, 0, 2))
    rims = pl.pallas_call(
        rims_kernel,
        out_shape=shape((288, 128), BF),
        in_specs=[vmem] * 3,
        out_specs=vmem,
        compiler_params=pltpu.CompilerParams(vmem_limit_bytes=8 << 20),
        cost_estimate=cost(0.5),
        name="rims",
    )(select, cells, solid_mask)
    rims_near = across(rims, 1)
    near = across(after(cells, weights), 1)

    odd = lax.axis_index("col") % 2 == 1
    low = lax.broadcasted_iota(jnp.int32, (144, 128), 1) < 64
    last = jnp.where(low, rims[:144], rims_near[144:])
    early = jnp.where(low, rims[144:], rims_near[:144])
    met_second = exchange(jnp.where(odd, last, early), 1)
    met_first = exchange(jnp.where(odd, early, last), 0)
    weights_far, weights_near = across(weights, 2), across(weights, 1)

    field_shape, rims_shape = shape((1920, 1024), BF), shape((4, 128, 128), F32)
    field, rim_cells, opened, open_rims, second, bias_second = pl.pallas_call(
        near_kernel,
        out_shape=[field_shape, rims_shape, shape((8, 1024), F32), shape((8, 128), F32), shape((288, 256), BF), shape((16, 128), F32)],
        in_specs=[vmem] * 5,
        out_specs=[vmem] * 6,
        compiler_params=pltpu.CompilerParams(vmem_limit_bytes=16 << 20),
        cost_estimate=cost(0.1),
        name="near",
    )(bias_two.reshape(1, 16), cells, near, solid_mask, weight_two.transpose(1, 0, 2))

    far = after(far, open_rims)
    cross = across(far, 1)
    field, rim_cells = pl.pallas_call(
        far_kernel,
        out_shape=[field_shape, rims_shape],
        in_specs=[vmem] * 3,
        out_specs=[vmem] * 2,
        input_output_aliases={1: 0, 2: 1},
        compiler_params=pltpu.CompilerParams(vmem_limit_bytes=16 << 20),
        cost_estimate=cost(0.1),
        name="far",
    )(far, field, rim_cells)
    weights_far, rim_cells = lax.optimization_barrier((weights_far, rim_cells))
    weights_cross = across(weights_far, 1)

    met_second, met_first, rim_cells = lax.optimization_barrier((met_second, met_first, rim_cells))
    before = jnp.where(odd, met_first, met_second)
    after_it = jnp.where(odd, met_second, met_first)
    there = across(jnp.concatenate([before[:128], after_it[:128]], 0), 2)

    _, rim_cells, hidden, first, bias, edges = pl.pallas_call(
        one_kernel,
        out_shape=[field_shape, rims_shape, shape((640, 1024), BF), shape((384, 768), BF), shape((64, 128), F32), shape((768, 512), BF)],
        in_specs=[vmem] * 10,
        out_specs=[vmem] * 6,
        input_output_aliases={8: 0, 9: 1},
        compiler_params=pltpu.CompilerParams(vmem_limit_bytes=24 << 20),
        cost_estimate=cost(4),
        name="one",
    )(cross, weights, weights_near, weights_far, weights_cross, opened, before, after_it, field, rim_cells)

    result, _ = pl.pallas_call(
        two_kernel,
        out_shape=[shape((128, 1024), BF), shape((768, 512), BF)],
        in_specs=[vmem] * 12,
        out_specs=[pl.BlockSpec(memory_space=pltpu.HBM), vmem],
        input_output_aliases={11: 1},
        scratch_shapes=[
            pltpu.VMEM((256, 512), BF),
            pltpu.VMEM((256, 128), BF),
            pltpu.VMEM((128, 1024), F32),
            pltpu.VMEM((128, 1024), BF),
            pltpu.VMEM((128, 1024), BF),
            pltpu.SemaphoreType.DMA((2,)),
        ],
        compiler_params=pltpu.CompilerParams(vmem_limit_bytes=16 << 20),
        cost_estimate=cost(3),
        name="two",
    )(before, after_it, there, rim_cells, open_rims, first, bias, second, bias_second, opened, hidden, edges)
    return result.reshape(16, 8, 1, 1024)


def passed_along(block, axis, distance):
    devices = range(lax.axis_size(axis))
    route = [(i - distance, i) for i in devices if i - distance in devices]
    return lax.ppermute(block, axis, route)


def kernel_of(weight):
    outputs = weight.shape[0]
    inputs = weight.shape[2]
    return weight.reshape(outputs, 3, 3, 3, inputs).transpose(0, 4, 1, 2, 3)


def many_rows(features, solid_mask, weight_one, bias_one, weight_two, bias_two):
    cells = features.shape[3]
    columns = lax.axis_size("col")
    grid_z = min(8, columns)
    open_cells = (1 - solid_mask).astype(jnp.float32)

    def pad_columns(field):
        depth = field.shape[0]
        depth_x = field.shape[1]
        cube = field.reshape(depth, depth_x, CY, CZ)
        below = passed_along(cube[:, :, :, CZ - 1 :], "col", 1)
        above = passed_along(cube[:, :, :, :1], "col", -1)
        place = lax.axis_index("col") % grid_z
        below = jnp.where(place > 0, below, jnp.zeros_like(below))
        above = jnp.where(place < grid_z - 1, above, jnp.zeros_like(above))
        cube = jnp.concatenate([below, cube, above], axis=3)
        south = passed_along(cube[:, :, CY - 1 :, :], "col", grid_z)
        north = passed_along(cube[:, :, :1, :], "col", -grid_z)
        return jnp.concatenate([south, cube, north], axis=2)

    def pad_planes(framed):
        return jnp.pad(framed, ((0, 0), (1, 1), (0, 0), (0, 0)))

    def padded_inputs(field):
        whole = lax.all_gather(field, "ch", axis=0, tiled=True)
        framed = pad_columns(whole)
        return pad_planes(framed)

    def convolve(framed, weight):
        depth_x = framed.shape[1] - 2
        result = lax.conv_general_dilated(
            framed[None],
            kernel_of(weight),
            (1, 1, 1),
            "VALID",
            dimension_numbers=("NCDHW", "OIDHW", "NCDHW"),
            preferred_element_type=jnp.float32,
        )
        return result[0].reshape(weight.shape[0], depth_x, 1, cells)

    def finish(total, bias, opened):
        return (jnp.maximum(total + bias[:, None, None, None], 0.0) * opened[None]).astype(
            jnp.bfloat16
        )

    hidden = finish(convolve(padded_inputs(features), weight_one), bias_one, open_cells)
    total = convolve(padded_inputs(hidden), weight_two)
    return finish(total, bias_two, open_cells)


def on_device(*arguments):
    columns = lax.axis_size("col")
    return one_row(*arguments) if columns <= 8 and columns % 2 == 0 else many_rows(*arguments)


def solution(mesh):
    in_specs = (
        P("ch", None, "col", None),
        P(None, "col", None),
        P("ch", None, None),
        P("ch"),
        P("ch", None, None),
        P("ch"),
    )
    out_specs = P("ch", None, "col", None)
    return jax.shard_map(
        on_device, mesh=mesh, in_specs=in_specs, out_specs=out_specs, check_vma=False
    )
```
